512 devices in a mesh: gy: 64 (over y, z), gz: 8 (over x, core).
Axes of the slice: x: 4, y: 4, z: 16, core: 2. Of those that a mesh axis runs over, the one named last changes fastest.
Arguments:
- volume: float32 [512, 128, 512], P('gy', 'gz'), may hold values from -8 to 8
Outputs:
- smoothed_volume: float32 [512, 128, 512], P('gy', 'gz')
The draws below stay inside these ranges and needn't reach their ends.
All inputs are finite; a program needn't handle non-finite values.
Results may differ from the reference program's by a relative error of at most 0.0003.
Values sent between devices are 32-bit elements; how exact they have to be, the bound alone decides.
A program may use at most 64 MiB of HBM per device.

```python
import jax
import jax.numpy as jnp
from jax import lax

X = 512
TAU = 1024
NY = 512
NZ = 128


def draw_volume(key, part):
    shape = (NY, NZ, X)
    return jnp.clip(2.0 * jax.random.normal(key, shape, jnp.float32), -8.0, 8.0)


def setup_inputs(seed: int = 0) -> dict:
    seeds = jax.random.split(jax.random.key(seed), 2)
    volume = draw_volume(jax.random.fold_in(seeds[1], 71), 0)
    return dict(volume=volume)


contrast = 0.05
explicit_rate = 0.25


def smooth_along(values, direction):
    length = values.shape[direction]
    return (lax.slice_in_dim(values, 0, length - 2, axis=direction) + 2.0 * lax.slice_in_dim(values, 1, length - 1, axis=direction) + lax.slice_in_dim(values, 2, length, axis=direction)) * 0.25


def central_along(values, direction):
    length = values.shape[direction]
    return (lax.slice_in_dim(values, 2, length, axis=direction) - lax.slice_in_dim(values, 0, length - 2, axis=direction)) * 0.5


def tensor_fields(extended):
    padded = jnp.pad(extended, ((0, 0), (0, 0), (2, 2)))
    smooth = smooth_along(smooth_along(smooth_along(padded, 0), 1), 2)
    grad_y = central_along(smooth, 0)[:, 1:-1, 1:-1]
    grad_z = central_along(smooth, 1)[1:-1, :, 1:-1]
    grad_x = central_along(smooth, 2)[1:-1, 1:-1, :]
    weight = 1.0 / (grad_y * grad_y + grad_z * grad_z + grad_x * grad_x + contrast)
    return (1.0 - weight * grad_y * grad_y, 1.0 - weight * grad_z * grad_z, 1.0 - weight * grad_x * grad_x,
            -weight * grad_x * grad_y, -weight * grad_x * grad_z, -weight * grad_y * grad_z)


def pad_columns(values):
    return jnp.pad(values, ((0, 0), (0, 0), (1, 1)))


def shifted(values, offset):
    row_count = values.shape[0] - 2
    slab_count = values.shape[1] - 2
    column_count = values.shape[2] - 2
    return values[1 + offset[0]:1 + offset[0] + row_count, 1 + offset[1]:1 + offset[1] + slab_count, 1 + offset[2]:1 + offset[2] + column_count]


def offset_sum(start_offset, extra_offset, factor_sign):
    return tuple(first_part + factor_sign * second_part for first_part, second_part in zip(start_offset, extra_offset))


def explicit_step(volume, rimmed, tensor_xx, tensor_xy, tensor_xz, tensor_yz):
    column_flux = 0.5 * (tensor_xx[:, :, :-1] + tensor_xx[:, :, 1:]) * (volume[:, :, 1:] - volume[:, :, :-1])
    padded_flux = pad_columns(column_flux)
    change = padded_flux[:, :, 1:] - padded_flux[:, :, :-1]
    padded = pad_columns(rimmed)
    unit_steps = ((1, 0, 0), (0, 1, 0), (0, 0, 1))
    pairs = ((0, 1, tensor_yz), (1, 0, tensor_yz), (0, 2, tensor_xy), (2, 0, tensor_xy), (1, 2, tensor_xz), (2, 1, tensor_xz))
    for first_axis, second_axis, tensor_entry in pairs:
        spread = pad_columns(tensor_entry)
        forward_unit = unit_steps[first_axis]
        across = unit_steps[second_axis]
        behind = tuple(-member for member in forward_unit)
        forward_part = shifted(spread, forward_unit) * (shifted(padded, offset_sum(forward_unit, across, 1)) - shifted(padded, offset_sum(forward_unit, across, -1)))
        backward_part = shifted(spread, behind) * (shifted(padded, offset_sum(behind, across, 1)) - shifted(padded, offset_sum(behind, across, -1)))
        change = change + 0.25 * (forward_part - backward_part)
    return volume + explicit_rate * change


def line_thomas(lower_cond, upper_cond, right_side):
    lower_band = -2.0 * TAU * lower_cond
    upper_band = -2.0 * TAU * upper_cond
    main_band = 1.0 - lower_band - upper_band

    def forward(carried, row_data):
        ratio_prev, value_prev = carried
        lower_here, main_here, upper_here, right_here = row_data
        inverse = 1.0 / (main_here - lower_here * ratio_prev)
        ratio_new = upper_here * inverse
        value_new = (right_here - lower_here * value_prev) * inverse
        return (ratio_new, value_new), (ratio_new, value_new)

    start_state = (jnp.zeros_like(right_side[0]), jnp.zeros_like(right_side[0]))
    _, (ratios, values) = lax.scan(forward, start_state, (lower_band, main_band, upper_band, right_side))

    def backward(next_value, row_data):
        ratio_here, value_here = row_data
        solved = value_here - ratio_here * next_value
        return solved, solved

    _, solution = lax.scan(backward, jnp.zeros_like(right_side[0]), (ratios, values), reverse=True)
    return solution


def reference(volume):
    extended = jnp.pad(volume, ((2, 2), (2, 2), (0, 0)))
    fields = tensor_fields(extended)
    rim = ((1, 1), (1, 1), (0, 0))
    rimmed = jnp.pad(volume, rim)
    explicit = explicit_step(volume, rimmed, fields[2], jnp.pad(fields[3], rim), jnp.pad(fields[4], rim), jnp.pad(fields[5], rim))
    conduct_y = 0.5 * (fields[0][:-1] + fields[0][1:])
    zero_row = jnp.zeros_like(conduct_y[:1])
    solve_y = line_thomas(jnp.concatenate([zero_row, conduct_y], 0), jnp.concatenate([conduct_y, zero_row], 0), explicit)
    conduct_z = 0.5 * (fields[1][:, :-1] + fields[1][:, 1:])
    zero_slab = jnp.zeros_like(conduct_z[:, :1])
    lower_z = jnp.moveaxis(jnp.concatenate([zero_slab, conduct_z], 1), 1, 0)
    upper_z = jnp.moveaxis(jnp.concatenate([conduct_z, zero_slab], 1), 1, 0)
    solve_z = jnp.moveaxis(line_thomas(lower_z, upper_z, jnp.moveaxis(explicit, 1, 0)), 0, 1)
    return 0.5 * (solve_y + solve_z)
```

```python
import functools

import jax
import jax.numpy as jnp
from jax import lax
from jax.experimental import pallas as pl
from jax.experimental.pallas import tpu as pltpu
from jax.sharding import PartitionSpec as P

TAU = 1024.0
CONTRAST = 0.05
RATE = 0.25

NY, NZ = 8, 16
HZ = NZ // 2
W = 3
GROUP = 16
GROUPS = 4
GZ = 8
LANES = 128
MESH = pl.DeviceIdType.MESH
f32 = jnp.float32


def lane_of(v):
    return lax.broadcasted_iota(jnp.int32, v.shape, v.ndim - 1)


def piece_of(v):
    return lax.broadcasted_iota(jnp.int32, v.shape, v.ndim - 2) % 4


def x_next(v, beyond=0.0):
    r = pltpu.roll(v, LANES - 1, v.ndim - 1)
    s = pltpu.roll(r, 7, v.ndim - 2)
    s = jnp.where(piece_of(v) == 3, beyond, s)
    return jnp.where(lane_of(v) == LANES - 1, s, r)


def x_prev(v, beyond=0.0):
    r = pltpu.roll(v, 1, v.ndim - 1)
    s = pltpu.roll(r, 1, v.ndim - 2)
    s = jnp.where(piece_of(v) == 0, beyond, s)
    return jnp.where(lane_of(v) == 0, s, r)


def join(block, after):
    a, b, d, f, g = block
    a2, b2, d2, f2, g2 = after
    m = d + a2
    inv = 1.0 / (b + b2 + m)
    t, w, h = b * inv, b2 * inv, g + f2
    return (a + t * m, t * b2, d2 + w * m, f + t * h, g2 + w * h), (h * inv, t, w)


def chain(blocks):
    total, steps = blocks[0], []
    for block in blocks[1:]:
        total, step = join(total, block)
        steps.append(step)
    return total, steps


def kernel(
    vol,
    out,
    ext,
    vp,
    sm,
    cy,
    cz,
    hy,
    base,
    sav_y,
    sav_z,
    out_y,
    in_y,
    out_z,
    in_z,
    out_s,
    in_s,
    sup,
    sep_y,
    sep_z,
    back_y,
    back_z,
    own_sem,
    halo_s,
    halo_r,
    y_s,
    y_r,
    z_s,
    z_r,
    s_s,
    s_r,
    by_s,
    by_r,
    bz_s,
    bz_r,
):
    gy, gz = lax.axis_index("gy"), lax.axis_index("gz")
    total_y = GROUP * GROUPS
    group, place = gy // GROUP, gy % GROUP

    around = [(i, j) for i in (-1, 0, 1) for j in (-1, 0, 1) if (i, j) != (0, 0)]
    ring = [8, 7, 9, 6, 10, 5, 11, 4, 12, 3, 13, 2, 14, 1, 15]

    def near(i, j):
        return ((gy + i + total_y) % total_y, (gz + j + GZ) % GZ)

    def in_ring(d):
        return (group * GROUP + (place + d) % GROUP, gz)

    def in_groups(d):
        return (((group + d) % GROUPS) * GROUP + place, gz)

    def in_gz(d):
        return (gy, (gz + d) % GZ)

    barrier = pltpu.get_barrier_semaphore()
    peers = [near(i, j) for i, j in around]
    peers += [in_ring(d) for d in ring]
    peers += [in_groups(d) for d in range(1, GROUPS)]
    peers += [in_gz(d) for d in range(1, GZ)]
    for peer in peers:
        pl.semaphore_signal(barrier, inc=1, device_id=peer, device_id_type=MESH)
    own = pltpu.make_async_copy(vol, ext.at[W : W + NY, W : W + NZ], own_sem)
    own.start()
    pl.semaphore_wait(barrier, len(peers))

    def src_range(i, n):
        return slice(n - W, n) if i > 0 else slice(0, W) if i < 0 else slice(0, n)

    def dst_range(i, n):
        return slice(0, W) if i > 0 else slice(W + n, n + 2 * W) if i < 0 else slice(W, W + n)

    halos = []
    for q, (i, j) in enumerate(around):
        copy = pltpu.make_async_remote_copy(
            src_ref=vol.at[src_range(i, NY), src_range(j, NZ)],
            dst_ref=ext.at[dst_range(i, NY), dst_range(j, NZ)],
            send_sem=halo_s.at[q],
            recv_sem=halo_r.at[q],
            device_id=near(i, j),
            device_id_type=MESH,
        )
        copy.start()
        halos.append(copy)
    own.wait()
    for copy in halos:
        copy.wait()

    @pl.when(gy == 0)
    def _():
        ext[0:W] = jnp.zeros((W, NZ + 2 * W, 4, LANES), f32)

    @pl.when(gy == total_y - 1)
    def _():
        ext[W + NY :] = jnp.zeros((W, NZ + 2 * W, 4, LANES), f32)

    @pl.when(gz == 0)
    def _():
        ext[:, 0:W] = jnp.zeros((NY + 2 * W, W, 4, LANES), f32)

    @pl.when(gz == GZ - 1)
    def _():
        ext[:, W + NZ :] = jnp.zeros((NY + 2 * W, W, 4, LANES), f32)

    def pack(r, carry):
        row = ext[r]
        vp[r] = jnp.concatenate([row[: HZ + 2 * W], row[HZ:]], axis=1)
        return carry

    lax.fori_loop(0, NY + 2 * W, pack, 0)

    def smooth(r, carry):
        v = vp[r] + 2.0 * vp[r + 1] + vp[r + 2]
        v = v[:-2] + 2.0 * v[1:-1] + v[2:]
        sm[0, r] = v
        sm[1, r] = x_prev(v) + 2.0 * v + x_next(v)
        return carry

    lax.fori_loop(0, NY + 4, smooth, 0)

    half = lax.broadcasted_iota(jnp.int32, (1, 8, LANES), 1) // 4
    low_in = jnp.where((half == 0) & (gz == 0), 0.0, 1.0).astype(f32)
    high_in = jnp.where((half == 1) & (gz == GZ - 1), 0.0, 1.0).astype(f32)

    def row_work(r, own_row, inside):
        mid = sm[1, r + 1]
        g_y = (sm[1, r + 2] - sm[1, r])[1:-1]
        g_z = mid[2:] - mid[:-2]
        core, filt = mid[1:-1], sm[0, r + 1][1:-1]
        g_x = x_next(core, filt) - x_prev(core, filt)
        yy, zz, xx = g_y * g_y, g_z * g_z, g_x * g_x
        small = f32(CONTRAST * 128.0 * 128.0)
        weight = 1.0 / (yy + zz + xx + small)
        off = weight
        if inside is not None:
            off = off * inside
        off = jnp.concatenate([off[:1] * low_in, off[1:-1], off[-1:] * high_in], axis=0)
        cy[r] = ((zz + xx + small) * weight)[1:-1]
        t_yz, t_xy = -off * g_y * g_z, -off * g_x * g_y
        v = vp[r + 2][2:-2]
        v_n = x_next(v)
        d_x = v_n - x_prev(v)
        v_z = vp[r + 2]
        d_z = (v_z[4:-2] - v_z[2:-4])
        hy[r] = t_xy[1:-1] * d_x[1:-1] + t_yz[1:-1] * d_z
        if own_row:
            t_xz = -off * g_x * g_z
            cz[r - 1] = ((yy + xx + small) * weight)[:-1]
            d_y = vp[r + 3][2:-2] - vp[r + 1][2:-2]
            k = t_xz * d_x + t_yz * d_y
            j = t_xy[1:-1] * d_y[1:-1] + t_xz[1:-1] * d_z
            t_xx = ((yy + zz + small) * weight)[1:-1]
            vc = v[1:-1]
            flux = 0.5 * (t_xx + x_next(t_xx)) * (v_n[1:-1] - vc)
            last = (lane_of(flux) == LANES - 1) & (piece_of(flux) == 3)
            flux = jnp.where(last, 0.0, flux)
            j = 0.25 * j
            change = (flux + x_next(j)) - x_prev(flux + j) + 0.25 * (k[2:] - k[:-2])
            base[r - 1] = vc + RATE * change

    def keep(cond):
        return jnp.where(cond, 0.0, 1.0).astype(f32)

    row_work(0, False, keep(gy == 0))
    row_work(NY + 1, False, keep(gy == total_y - 1))

    def own_rows(r, carry):
        row_work(r, True, None)
        return carry

    lax.fori_loop(1, NY + 1, own_rows, 0)

    def finish(r, carry):
        base[r] = base[r] + (RATE * 0.25) * (hy[r + 2] - hy[r])
        return carry

    lax.fori_loop(0, NY, finish, 0)

    def reduce(first, link, right, save):
        a, b, d, f, g = jnp.zeros_like(first), first, jnp.ones_like(first), jnp.zeros_like(first), right(0)
        for s in range(1, 8):
            c = link(s)
            inv = 1.0 / (b + c + d)
            t, w = b * inv, c * inv
            save[s - 1, 0], save[s - 1, 1], save[s - 1, 2] = g * inv, t, w
            a, f = a + t * d, f + t * g
            b, d, g = t * c, 1.0 + w * d, right(s) + w * g
        return a, b, d, f, g

    first_y = TAU * (cy[0] + cy[1]) * keep(gy == 0)
    port = reduce(first_y, lambda s: TAU * (cy[s] + cy[s + 1]), lambda s: base[s], sav_y)
    for c, part in enumerate(port):
        out_y[0:HZ, c] = part[:, 0:4]
        out_y[HZ:, c] = part[:, 4:8]

    first_z = TAU * (cz[:, 0] + cz[:, 1]) * low_in
    port = reduce(first_z, lambda s: TAU * (cz[:, s] + cz[:, s + 1]), lambda s: base[:, s], sav_z)
    for c, part in enumerate(port):
        out_z[:, c] = part

    y_copies, z_copies = [], []
    for d in ring:
        copy = pltpu.make_async_remote_copy(
            src_ref=out_y.at[(place + d) % GROUP],
            dst_ref=in_y.at[place],
            send_sem=y_s.at[d - 1],
            recv_sem=y_r.at[d - 1],
            device_id=in_ring(d),
            device_id_type=MESH,
        )
        copy.start()
        y_copies.append(copy)
    for d in range(1, GZ):
        copy = pltpu.make_async_remote_copy(
            src_ref=out_z.at[(gz + d) % GZ],
            dst_ref=in_z.at[gz],
            send_sem=z_s.at[d - 1],
            recv_sem=z_r.at[d - 1],
            device_id=in_gz(d),
            device_id_type=MESH,
        )
        copy.start()
        z_copies.append(copy)
    in_y[place] = out_y[place]
    in_z[gz] = out_z[gz]

    for copy in y_copies:
        copy.wait()
    total, steps = chain([tuple(in_y[k, c] for c in range(5)) for k in range(GROUP)])
    for c in range(5):
        out_s[c] = total[c]
        in_s[group, c] = total[c]
    s_copies = []
    for d in range(1, GROUPS):
        copy = pltpu.make_async_remote_copy(
            src_ref=out_s,
            dst_ref=in_s.at[group],
            send_sem=s_s.at[d - 1],
            recv_sem=s_r.at[d - 1],
            device_id=in_groups(d),
            device_id_type=MESH,
        )
        copy.start()
        s_copies.append(copy)

    for copy in z_copies:
        copy.wait()
    blocks = [tuple(in_z[k // 2, c, 4 * (k % 2) : 4 * (k % 2) + 4] for c in range(5)) for k in range(2 * GZ)]
    whole, z_steps = chain(blocks)
    u = whole[4] / (whole[1] + whole[2])
    sep_z[0] = jnp.zeros((4, LANES), f32)
    sep_z[2 * GZ] = u
    for k in reversed(range(2 * GZ - 1)):
        h, _, w = z_steps[k]
        u = h + w * u
        sep_z[k + 1] = u
    bz_copies = []
    for d in range(1, GZ):
        copy = pltpu.make_async_remote_copy(
            src_ref=sep_z.at[pl.ds(2 * ((gz + d) % GZ), 3)],
            dst_ref=back_z.at[gz],
            send_sem=bz_s.at[d - 1],
            recv_sem=bz_r.at[d - 1],
            device_id=in_gz(d),
            device_id_type=MESH,
        )
        copy.start()
        bz_copies.append(copy)
    back_z[gz] = sep_z[pl.ds(2 * gz, 3)]

    for copy in s_copies:
        copy.wait()
    whole, s_steps = chain([tuple(in_s[k, c] for c in range(5)) for k in range(GROUPS)])
    u = whole[4] / (whole[1] + whole[2])
    sup[0] = jnp.zeros((4, LANES), f32)
    sup[GROUPS] = u
    for k in reversed(range(GROUPS - 1)):
        h, _, w = s_steps[k]
        u = h + w * u
        sup[k + 1] = u
    before, u = sup[group], sup[group + 1]
    sep_y[0], sep_y[GROUP] = before, u
    for k in reversed(range(GROUP - 1)):
        h, t, w = steps[k]
        u = h + t * before + w * u
        sep_y[k + 1] = u
    by_copies = []
    for d in ring:
        copy = pltpu.make_async_remote_copy(
            src_ref=sep_y.at[pl.ds((place + d) % GROUP, 2)],
            dst_ref=back_y.at[place],
            send_sem=by_s.at[d - 1],
            recv_sem=by_r.at[d - 1],
            device_id=in_ring(d),
            device_id_type=MESH,
        )
        copy.start()
        by_copies.append(copy)
    back_y[place] = sep_y[pl.ds(place, 2)]

    for copy in bz_copies:
        copy.wait()
    before = jnp.concatenate([back_z[:, 0], back_z[:, 1]], axis=1)
    u = jnp.concatenate([back_z[:, 1], back_z[:, 2]], axis=1)
    base[:, HZ - 1] = u
    for s in reversed(range(HZ - 1)):
        u = sav_z[s, 0] + sav_z[s, 1] * before + sav_z[s, 2] * u
        base[:, s] = u

    for copy in by_copies:
        copy.wait()
    before = jnp.concatenate([back_y[0:HZ, 0], back_y[HZ:, 0]], axis=1)
    u = jnp.concatenate([back_y[0:HZ, 1], back_y[HZ:, 1]], axis=1)
    for s in reversed(range(NY)):
        if s < NY - 1:
            u = sav_y[s, 0] + sav_y[s, 1] * before + sav_y[s, 2] * u
        both = 0.5 * (u + base[s])
        out[s, 0:HZ] = both[:, 0:4]
        out[s, HZ:] = both[:, 4:8]


def per_device(volume):
    vm = lambda *shape: pltpu.VMEM(shape, f32)
    sem = lambda n: pltpu.SemaphoreType.DMA((n,))
    full = (8, LANES)
    part = (4, LANES)
    result = pl.pallas_call(
        kernel,
        out_shape=jax.ShapeDtypeStruct((NY, NZ) + part, f32),
        in_specs=[pl.BlockSpec(memory_space=pltpu.VMEM)],
        out_specs=pl.BlockSpec(memory_space=pltpu.VMEM),
        scratch_shapes=[
            vm(NY + 2 * W, NZ + 2 * W, *part),
            vm(NY + 2 * W, HZ + 2 * W, *full),
            vm(2, NY + 4, HZ + 4, *full),
            vm(NY + 2, HZ, *full),
            vm(NY, HZ + 1, *full),
            vm(NY + 2, HZ, *full),
            vm(NY, HZ, *full),
            vm(NY - 1, 3, HZ, *full),
            vm(HZ - 1, 3, NY, *full),
            vm(GROUP, 5, *part),
            vm(GROUP, 5, *part),
            vm(GZ, 5, *full),
            vm(GZ, 5, *full),
            vm(5, *part),
            vm(GROUPS, 5, *part),
            vm(GROUPS + 1, *part),
            vm(GROUP + 1, *part),
            vm(2 * GZ + 1, *part),
            vm(GROUP, 2, *part),
            vm(GZ, 3, *part),
            pltpu.SemaphoreType.DMA,
            sem(8),
            sem(8),
            sem(GROUP - 1),
            sem(GROUP - 1),
            sem(GZ - 1),
            sem(GZ - 1),
            sem(GROUPS - 1),
            sem(GROUPS - 1),
            sem(GROUP - 1),
            sem(GROUP - 1),
            sem(GZ - 1),
            sem(GZ - 1),
        ],
        compiler_params=pltpu.CompilerParams(
            collective_id=0, has_side_effects=True, vmem_limit_bytes=32 * 1024 * 1024
        ),
        name="diffusion_step",
    )(volume.reshape((NY, NZ) + part))
    return result.reshape(volume.shape)


def solution(mesh):
    placed = P("gy", "gz", None)
    return jax.shard_map(
        per_device, mesh=mesh, in_specs=(placed,), out_specs=placed, check_vma=False
    )
```

```python
import functools

import jax
import jax.numpy as jnp
from jax import lax
from jax.experimental import pallas as pl
from jax.experimental.pallas import tpu as pltpu
from jax.sharding import PartitionSpec as P

TAU = 1024.0
CONTRAST = 0.05
RATE = 0.25

NY, NZ = 8, 16
HZ = NZ // 2
W = 3
GROUP = 16
GROUPS = 4
GZ = 8
LANES = 128
MESH = pl.DeviceIdType.MESH
f32 = jnp.float32


def lane_of(v):
    return lax.broadcasted_iota(jnp.int32, v.shape, v.ndim - 1)


def piece_of(v):
    return lax.broadcasted_iota(jnp.int32, v.shape, v.ndim - 2) % 4


def x_next(v, beyond=0.0):
    r = pltpu.roll(v, LANES - 1, v.ndim - 1)
    s = pltpu.roll(r, 7, v.ndim - 2)
    s = jnp.where(piece_of(v) == 3, beyond, s)
    return jnp.where(lane_of(v) == LANES - 1, s, r)


def x_prev(v, beyond=0.0):
    r = pltpu.roll(v, 1, v.ndim - 1)
    s = pltpu.roll(r, 1, v.ndim - 2)
    s = jnp.where(piece_of(v) == 0, beyond, s)
    return jnp.where(lane_of(v) == 0, s, r)


def join(block, after):
    a, b, d, f, g = block
    a2, b2, d2, f2, g2 = after
    m = d + a2
    inv = 1.0 / (b + b2 + m)
    t, w, h = b * inv, b2 * inv, g + f2
    return (a + t * m, t * b2, d2 + w * m, f + t * h, g2 + w * h), (h * inv, t, w)


def chain(blocks):
    total, steps = blocks[0], []
    for block in blocks[1:]:
        total, step = join(total, block)
        steps.append(step)
    return total, steps


def kernel(
    vol,
    out,
    raw,
    ext,
    vp,
    sm,
    cy,
    cz,
    hy,
    base,
    sav_y,
    sav_z,
    out_y,
    in_y,
    out_z,
    in_z,
    out_b,
    sep_z,
    back_y,
    back_z,
    own_sem,
    halo_s,
    halo_r,
    y_s,
    y_r,
    z_s,
    z_r,
    known,
    by_s,
    by_r,
    bz_s,
    bz_r,
):
    gy, gz = lax.axis_index("gy"), lax.axis_index("gz")
    total_y = GROUP * GROUPS
    group, place = gy // GROUP, gy % GROUP

    around = [(0, -1), (0, 1), (-1, 0), (1, 0), (-1, -1), (-1, 1), (1, -1), (1, 1)]
    ring = [8, 7, 9, 6, 10, 5, 11, 4, 12, 3, 13, 2, 14, 1, 15]
    line = [(e, d) for d in ring + [0] for e in (2, 1, 3, 0) if (e, d) != (0, 0)]

    def near(i, j):
        return ((gy + i + total_y) % total_y, (gz + j + GZ) % GZ)

    def in_line(e, d):
        return (group + e) % GROUPS, (place + d) % GROUP

    def in_gz(d):
        return (gy, (gz + d) % GZ)

    def at(q, k):
        return (q * GROUP + k, gz)

    barrier = pltpu.get_barrier_semaphore()
    peers = [near(i, j) for i, j in around[2:]]
    peers += [at(*in_line(0, d)) for d in ring]
    peers += [in_gz(d) for d in range(1, GZ)]
    peers += [at(*in_line(e, 0)) for e in range(1, GROUPS)]
    for peer in peers:
        pl.semaphore_signal(barrier, inc=1, device_id=peer, device_id_type=MESH)
    own = pltpu.make_async_copy(vol, raw, own_sem)
    own.start()
    own.wait()

    def relay(r, carry):
        for t in range(4):
            ext[r + W, W : W + NZ, t] = raw[r, :, t * LANES : (t + 1) * LANES]
        return carry

    lax.fori_loop(0, NY, relay, 0)
    pl.semaphore_wait(barrier, len(peers))

    def src_range(i, n):
        return slice(n, n + W) if i > 0 else slice(W, 2 * W) if i < 0 else slice(W, W + n)

    def dst_range(i, n):
        return slice(0, W) if i > 0 else slice(W + n, n + 2 * W) if i < 0 else slice(W, W + n)

    halos = []
    for q, (i, j) in enumerate(around):
        copy = pltpu.make_async_remote_copy(
            src_ref=ext.at[src_range(i, NY), src_range(j, NZ)],
            dst_ref=ext.at[dst_range(i, NY), dst_range(j, NZ)],
            send_sem=halo_s.at[q],
            recv_sem=halo_r.at[q],
            device_id=near(i, j),
            device_id_type=MESH,
        )
        copy.start()
        halos.append(copy)
    for e in range(1, GROUPS):
        pl.semaphore_signal(known, inc=1, device_id=at(*in_line(e, 0)), device_id_type=MESH)

    def pack(r):
        row = ext[r]
        vp[r] = jnp.concatenate([row[: HZ + 2 * W], row[HZ:]], axis=1)

    def smooth(r):
        v = vp[r] + 2.0 * vp[r + 1] + vp[r + 2]
        v = v[:-2] + 2.0 * v[1:-1] + v[2:]
        sm[0, r] = v
        sm[1, r] = x_prev(v) + 2.0 * v + x_next(v)

    half = lax.broadcasted_iota(jnp.int32, (1, 8, LANES), 1) // 4
    low_in = jnp.where((half == 0) & (gz == 0), 0.0, 1.0).astype(f32)
    high_in = jnp.where((half == 1) & (gz == GZ - 1), 0.0, 1.0).astype(f32)

    def row_work(r, own_row, inside):
        mid = sm[1, r + 1]
        g_y = (sm[1, r + 2] - sm[1, r])[1:-1]
        g_z = mid[2:] - mid[:-2]
        core, filt = mid[1:-1], sm[0, r + 1][1:-1]
        g_x = x_next(core, filt) - x_prev(core, filt)
        yy, zz, xx = g_y * g_y, g_z * g_z, g_x * g_x
        small = f32(CONTRAST * 128.0 * 128.0)
        weight = 1.0 / (yy + zz + xx + small)
        off = weight
        if inside is not None:
            off = off * inside
        off = jnp.concatenate([off[:1] * low_in, off[1:-1], off[-1:] * high_in], axis=0)
        cy[r] = ((zz + xx + small) * weight)[1:-1]
        t_yz, t_xy = -off * g_y * g_z, -off * g_x * g_y
        v = vp[r + 2][2:-2]
        v_n = x_next(v)
        d_x = v_n - x_prev(v)
        v_z = vp[r + 2]
        d_z = (v_z[4:-2] - v_z[2:-4])
        hy[r] = t_xy[1:-1] * d_x[1:-1] + t_yz[1:-1] * d_z
        if own_row:
            t_xz = -off * g_x * g_z
            cz[r - 1] = ((yy + xx + small) * weight)[:-1]
            d_y = vp[r + 3][2:-2] - vp[r + 1][2:-2]
            k = t_xz * d_x + t_yz * d_y
            j = t_xy[1:-1] * d_y[1:-1] + t_xz[1:-1] * d_z
            t_xx = ((yy + zz + small) * weight)[1:-1]
            vc = v[1:-1]
            flux = 0.5 * (t_xx + x_next(t_xx)) * (v_n[1:-1] - vc)
            last = (lane_of(flux) == LANES - 1) & (piece_of(flux) == 3)
            flux = jnp.where(last, 0.0, flux)
            j = 0.25 * j
            change = (flux + x_next(j)) - x_prev(flux + j) + 0.25 * (k[2:] - k[:-2])
            base[r - 1] = vc + RATE * change

    def keep(cond):
        return jnp.where(cond, 0.0, 1.0).astype(f32)

    def rows(count, row, work):
        def body(n, carry):
            work(row(n))
            return carry

        lax.fori_loop(0, count, body, 0)

    def own_row(r):
        row_work(r, True, None)

    for copy in halos[:2]:
        copy.wait()

    @pl.when(gz == 0)
    def _():
        ext[W : W + NY, 0:W] = jnp.zeros((NY, W, 4, LANES), f32)

    @pl.when(gz == GZ - 1)
    def _():
        ext[W : W + NY, W + NZ :] = jnp.zeros((NY, W, 4, LANES), f32)

    rows(NY, lambda n: n + W, pack)
    rows(NY - 2, lambda n: n + 3, smooth)
    rows(NY - 4, lambda n: n + 3, own_row)

    for copy in halos[2:]:
        copy.wait()

    @pl.when(gy == 0)
    def _():
        ext[0:W] = jnp.zeros((W, NZ + 2 * W, 4, LANES), f32)

    @pl.when(gy == total_y - 1)
    def _():
        ext[W + NY :] = jnp.zeros((W, NZ + 2 * W, 4, LANES), f32)

    @pl.when(gz == 0)
    def _():
        for first in (0, W + NY):
            ext[first : first + W, 0:W] = jnp.zeros((W, W, 4, LANES), f32)

    @pl.when(gz == GZ - 1)
    def _():
        for first in (0, W + NY):
            ext[first : first + W, W + NZ :] = jnp.zeros((W, W, 4, LANES), f32)

    rows(2 * W, lambda n: n + NY * (n // 3), pack)
    rows(6, lambda n: n + 6 * (n // 3), smooth)
    row_work(0, False, keep(gy == 0))
    row_work(NY + 1, False, keep(gy == total_y - 1))
    rows(4, lambda n: n + 1 + 4 * (n // 2), own_row)

    def reduce(first, link, right, save):
        a, b, d, f, g = jnp.zeros_like(first), first, jnp.ones_like(first), jnp.zeros_like(first), right(0)
        for s in range(1, 8):
            c = link(s)
            inv = 1.0 / (b + c + d)
            t, w = b * inv, c * inv
            save[s - 1, 0], save[s - 1, 1], save[s - 1, 2] = g * inv, t, w
            a, f = a + t * d, f + t * g
            b, d, g = t * c, 1.0 + w * d, right(s) + w * g
        return a, b, d, f, g

    def explicit(s):
        now = base[s] + (RATE * 0.25) * (hy[s + 2] - hy[s])
        base[s] = now
        return now

    first_y = TAU * (cy[0] + cy[1]) * keep(gy == 0)
    port = reduce(first_y, lambda s: TAU * (cy[s] + cy[s + 1]), explicit, sav_y)
    for c, part in enumerate(port):
        for k in range(HZ):
            out_y[k, :, c] = part[k]

    def slot(q, k):
        return k % HZ, (k // HZ) * 4 + q

    pl.semaphore_wait(known, GROUPS - 1)
    y_copies, z_copies = [], []
    for n, (e, d) in enumerate(line):
        q, k = in_line(e, d)
        copy = pltpu.make_async_remote_copy(
            src_ref=out_y.at[slot(q, k)],
            dst_ref=in_y.at[gy // 8, gy % 8],
            send_sem=y_s.at[n],
            recv_sem=y_r.at[n],
            device_id=at(q, k),
            device_id_type=MESH,
        )
        copy.start()
        y_copies.append(copy)
    in_y[gy // 8, gy % 8] = out_y[slot(group, place)]

    first_z = TAU * (cz[:, 0] + cz[:, 1]) * low_in
    port = reduce(first_z, lambda s: TAU * (cz[:, s] + cz[:, s + 1]), lambda s: base[:, s], sav_z)
    for c, part in enumerate(port):
        out_z[:, c] = part
    for d in range(1, GZ):
        copy = pltpu.make_async_remote_copy(
            src_ref=out_z.at[(gz + d) % GZ],
            dst_ref=in_z.at[gz],
            send_sem=z_s.at[d - 1],
            recv_sem=z_r.at[d - 1],
            device_id=in_gz(d),
            device_id_type=MESH,
        )
        copy.start()
        z_copies.append(copy)
    in_z[gz] = out_z[gz]

    for copy in z_copies:
        copy.wait()
    blocks = [tuple(in_z[k // 2, c, 4 * (k % 2) : 4 * (k % 2) + 4] for c in range(5)) for k in range(2 * GZ)]
    whole, z_steps = chain(blocks)
    u = whole[4] / (whole[1] + whole[2])
    sep_z[0] = jnp.zeros((4, LANES), f32)
    sep_z[2 * GZ] = u
    for k in reversed(range(2 * GZ - 1)):
        h, _, w = z_steps[k]
        u = h + w * u
        sep_z[k + 1] = u
    bz_copies = []
    for d in range(1, GZ):
        copy = pltpu.make_async_remote_copy(
            src_ref=sep_z.at[pl.ds(2 * ((gz + d) % GZ), 3)],
            dst_ref=back_z.at[gz],
            send_sem=bz_s.at[d - 1],
            recv_sem=bz_r.at[d - 1],
            device_id=in_gz(d),
            device_id_type=MESH,
        )
        copy.start()
        bz_copies.append(copy)
    back_z[gz] = sep_z[pl.ds(2 * gz, 3)]

    for copy in y_copies:
        copy.wait()
    total, steps = chain([tuple(in_y[:, i, c] for c in range(5)) for i in range(8)])
    whole, run_steps = chain([tuple(part[s : s + 1] for part in total) for s in range(8)])
    u = whole[4] / (whole[1] + whole[2])
    ends = [u]
    for h, _, w in reversed(run_steps):
        u = h + w * u
        ends.insert(0, u)
    before = jnp.concatenate([jnp.zeros((1, LANES), f32)] + ends[:-1], axis=0)
    u = jnp.concatenate(ends, axis=0)
    out_b[:, 0, 0] = before
    out_b[:, 7, 1] = u
    for i in reversed(range(7)):
        h, t, w = steps[i]
        u = h + t * before + w * u
        out_b[:, i, 1] = u
        out_b[:, i + 1, 0] = u
    by_copies = []
    for n, (e, d) in enumerate(line):
        q, k = in_line(e, d)
        there = q * GROUP + k
        copy = pltpu.make_async_remote_copy(
            src_ref=out_b.at[there // 8, there % 8],
            dst_ref=back_y.at[slot(group, place)],
            send_sem=by_s.at[n],
            recv_sem=by_r.at[n],
            device_id=at(q, k),
            device_id_type=MESH,
        )
        copy.start()
        by_copies.append(copy)
    back_y[slot(group, place)] = out_b[gy // 8, gy % 8]

    for copy in bz_copies:
        copy.wait()
    before = jnp.concatenate([back_z[:, 0], back_z[:, 1]], axis=1)
    u = jnp.concatenate([back_z[:, 1], back_z[:, 2]], axis=1)
    base[:, HZ - 1] = u
    for s in reversed(range(HZ - 1)):
        u = sav_z[s, 0] + sav_z[s, 1] * before + sav_z[s, 2] * u
        base[:, s] = u

    for copy in by_copies:
        copy.wait()
    before, u = back_y[:, :, 0], back_y[:, :, 1]
    for s in reversed(range(NY)):
        if s < NY - 1:
            u = sav_y[s, 0] + sav_y[s, 1] * before + sav_y[s, 2] * u
        both = 0.5 * (u + base[s])
        out[s, 0:HZ] = both[:, 0:4]
        out[s, HZ:] = both[:, 4:8]


def per_device(volume):
    vm = lambda *shape: pltpu.VMEM(shape, f32)
    sem = lambda n: pltpu.SemaphoreType.DMA((n,))
    full = (8, LANES)
    part = (4, LANES)
    result = pl.pallas_call(
        kernel,
        out_shape=jax.ShapeDtypeStruct((NY, NZ) + part, f32),
        in_specs=[pl.BlockSpec(memory_space=pl.ANY)],
        out_specs=pl.BlockSpec(memory_space=pltpu.VMEM),
        scratch_shapes=[
            vm(NY, NZ, 4 * LANES),
            vm(NY + 2 * W, NZ + 2 * W, *part),
            vm(NY + 2 * W, HZ + 2 * W, *full),
            vm(2, NY + 4, HZ + 4, *full),
            vm(NY + 2, HZ, *full),
            vm(NY, HZ + 1, *full),
            vm(NY + 2, HZ, *full),
            vm(NY, HZ, *full),
            vm(NY - 1, 3, HZ, *full),
            vm(HZ - 1, 3, NY, *full),
            vm(HZ, 8, 5, LANES),
            vm(8, 8, 5, LANES),
            vm(GZ, 5, *full),
            vm(GZ, 5, *full),
            vm(8, 8, 2, LANES),
            vm(2 * GZ + 1, *part),
            vm(HZ, 8, 2, LANES),
            vm(GZ, 3, *part),
            pltpu.SemaphoreType.DMA,
            sem(8),
            sem(8),
            sem(GROUP * GROUPS - 1),
            sem(GROUP * GROUPS - 1),
            sem(GZ - 1),
            sem(GZ - 1),
            pltpu.SemaphoreType.REGULAR,
            sem(GROUP * GROUPS - 1),
            sem(GROUP * GROUPS - 1),
            sem(GZ - 1),
            sem(GZ - 1),
        ],
        compiler_params=pltpu.CompilerParams(
            collective_id=0, has_side_effects=True, vmem_limit_bytes=32 * 1024 * 1024
        ),
        name="diffusion_step",
    )(volume)
    return result.reshape(volume.shape)


def solution(mesh):
    placed = P("gy", "gz", None)
    return jax.shard_map(
        per_device, mesh=mesh, in_specs=(placed,), out_specs=placed, check_vma=False
    )
```

```python
import functools

import jax
import jax.numpy as jnp
from jax import lax
from jax.experimental import pallas as pl
from jax.experimental.pallas import tpu as pltpu
from jax.sharding import PartitionSpec as P

TAU = 1024.0
CONTRAST = 0.05
RATE = 0.25

NY, NZ = 8, 16
HZ = NZ // 2
W = 3
GROUP = 16
GROUPS = 4
GZ = 8
LANES = 128
MESH = pl.DeviceIdType.MESH
f32 = jnp.float32


def lane_of(v):
    return lax.broadcasted_iota(jnp.int32, v.shape, v.ndim - 1)


def piece_of(v):
    return lax.broadcasted_iota(jnp.int32, v.shape, v.ndim - 2) % 4


def x_next(v, beyond=0.0):
    r = pltpu.roll(v, LANES - 1, v.ndim - 1)
    s = pltpu.roll(r, 7, v.ndim - 2)
    s = jnp.where(piece_of(v) == 3, beyond, s)
    return jnp.where(lane_of(v) == LANES - 1, s, r)


def x_prev(v, beyond=0.0):
    r = pltpu.roll(v, 1, v.ndim - 1)
    s = pltpu.roll(r, 1, v.ndim - 2)
    s = jnp.where(piece_of(v) == 0, beyond, s)
    return jnp.where(lane_of(v) == 0, s, r)


def join(block, after):
    a, b, d, f, g = block
    a2, b2, d2, f2, g2 = after
    m = d + a2
    inv = 1.0 / (b + b2 + m)
    t, w, h = b * inv, b2 * inv, g + f2
    return (a + t * m, t * b2, d2 + w * m, f + t * h, g2 + w * h), (h * inv, t, w)


def chain(blocks):
    total, steps = blocks[0], []
    for block in blocks[1:]:
        total, step = join(total, block)
        steps.append(step)
    return total, steps


def kernel(
    vol,
    out,
    ext,
    vp,
    sm,
    cy,
    cz,
    hy,
    base,
    sav_y,
    sav_z,
    out_y,
    in_y,
    out_z,
    in_z,
    out_b,
    sep_z,
    back_y,
    back_z,
    own_sem,
    known,
    halo_y,
    halo_z,
    sem_y,
    sem_z,
    sem_by,
    sem_bz,
):
    gy, gz = lax.axis_index("gy"), lax.axis_index("gz")
    total_y = GROUP * GROUPS
    group, place = gy // GROUP, gy % GROUP

    around = [(0, -1), (0, 1), (-1, 0), (1, 0), (-1, -1), (-1, 1), (1, -1), (1, 1)]
    ring = [8, 7, 9, 6, 10, 5, 11, 4, 12, 3, 13, 2, 14, 1, 15]
    line = [(e, d) for d in ring + [0] for e in (2, 1, 3, 0) if (e, d) != (0, 0)]

    def wrapped(x, n):
        return jnp.where(x >= n, x - n, x)

    places = [wrapped(place + d, GROUP) for d in range(GROUP)]
    groups = [wrapped(group + e, GROUPS) for e in range(GROUPS)]
    gzs = [wrapped(gz + d, GZ) for d in range(GZ)]
    gys = [gy, wrapped(gy + 1, total_y), wrapped(gy + total_y - 1, total_y)]

    def at(e, d):
        return (groups[e] * GROUP + places[d], gz)

    def send(src, dst, sems, peer):
        pltpu.make_async_remote_copy(
            src_ref=src,
            dst_ref=dst,
            send_sem=sems.at[0],
            recv_sem=sems.at[1],
            device_id=peer,
            device_id_type=MESH,
        ).start()

    def keep_own(src, dst, sems):
        pltpu.make_async_copy(src, dst, sems.at[1]).start()

    def wait(ref, sem):
        pltpu.make_async_copy(ref, ref, sem).wait()

    for t in range(4):
        pltpu.make_async_copy(
            vol.at[:, :, t * LANES : (t + 1) * LANES], ext.at[W : W + NY, W : W + NZ, t], own_sem
        ).start()

    barrier = pltpu.get_barrier_semaphore()
    peers = [(gys[i], gzs[j]) for i, j in around[2:]]
    peers += [at(0, d) for d in ring]
    peers += [(gy, gzs[d]) for d in range(1, GZ)]
    peers += [at(e, 0) for e in range(1, GROUPS)]
    for peer in peers:
        pl.semaphore_signal(barrier, inc=1, device_id=peer, device_id_type=MESH)
    wait(ext.at[W : W + NY, W : W + NZ], own_sem)
    pl.semaphore_wait(barrier, len(peers))

    def src_range(i, n):
        return slice(n, n + W) if i > 0 else slice(W, 2 * W) if i < 0 else slice(W, W + n)

    def dst_range(i, n):
        return slice(0, W) if i > 0 else slice(W + n, n + 2 * W) if i < 0 else slice(W, W + n)

    for i, j in around:
        send(
            ext.at[src_range(i, NY), src_range(j, NZ)],
            ext.at[dst_range(i, NY), dst_range(j, NZ)],
            halo_z if i == 0 else halo_y,
            (gys[i], gzs[j]),
        )
    for e in range(1, GROUPS):
        pl.semaphore_signal(known, inc=1, device_id=at(e, 0), device_id_type=MESH)

    def pack(r):
        row = ext[r]
        vp[r] = jnp.concatenate([row[: HZ + 2 * W], row[HZ:]], axis=1)

    def smooth(r):
        v = vp[r] + 2.0 * vp[r + 1] + vp[r + 2]
        v = v[:-2] + 2.0 * v[1:-1] + v[2:]
        sm[0, r] = v
        sm[1, r] = x_prev(v) + 2.0 * v + x_next(v)

    half = lax.broadcasted_iota(jnp.int32, (1, 8, LANES), 1) // 4
    low_in = jnp.where((half == 0) & (gz == 0), 0.0, 1.0).astype(f32)
    high_in = jnp.where((half == 1) & (gz == GZ - 1), 0.0, 1.0).astype(f32)

    def row_work(r, own_row, inside):
        mid = sm[1, r + 1]
        g_y = (sm[1, r + 2] - sm[1, r])[1:-1]
        g_z = mid[2:] - mid[:-2]
        core, filt = mid[1:-1], sm[0, r + 1][1:-1]
        g_x = x_next(core, filt) - x_prev(core, filt)
        yy, zz, xx = g_y * g_y, g_z * g_z, g_x * g_x
        small = f32(CONTRAST * 128.0 * 128.0)
        weight = 1.0 / (yy + zz + xx + small)
        off = weight
        if inside is not None:
            off = off * inside
        off = jnp.concatenate([off[:1] * low_in, off[1:-1], off[-1:] * high_in], axis=0)
        cy[r] = ((zz + xx + small) * weight)[1:-1]
        t_yz, t_xy = -off * g_y * g_z, -off * g_x * g_y
        v = vp[r + 2][2:-2]
        v_n = x_next(v)
        d_x = v_n - x_prev(v)
        v_z = vp[r + 2]
        d_z = (v_z[4:-2] - v_z[2:-4])
        hy[r] = t_xy[1:-1] * d_x[1:-1] + t_yz[1:-1] * d_z
        if own_row:
            t_xz = -off * g_x * g_z
            cz[r - 1] = ((yy + xx + small) * weight)[:-1]
            d_y = vp[r + 3][2:-2] - vp[r + 1][2:-2]
            k = t_xz * d_x + t_yz * d_y
            j = t_xy[1:-1] * d_y[1:-1] + t_xz[1:-1] * d_z
            t_xx = ((yy + zz + small) * weight)[1:-1]
            vc = v[1:-1]
            flux = 0.5 * (t_xx + x_next(t_xx)) * (v_n[1:-1] - vc)
            last = (lane_of(flux) == LANES - 1) & (piece_of(flux) == 3)
            flux = jnp.where(last, 0.0, flux)
            j = 0.25 * j
            change = (flux + x_next(j)) - x_prev(flux + j) + 0.25 * (k[2:] - k[:-2])
            base[r - 1] = vc + RATE * change

    def keep(cond):
        return jnp.where(cond, 0.0, 1.0).astype(f32)

    def rows(count, row, work):
        def body(n, carry):
            work(row(n))
            return carry

        lax.fori_loop(0, count, body, 0)

    def own_row(r):
        row_work(r, True, None)

    wait(ext.at[W : W + NY, 0 : 2 * W], halo_z.at[1])

    @pl.when(gz == 0)
    def _():
        ext[W : W + NY, 0:W] = jnp.zeros((NY, W, 4, LANES), f32)

    @pl.when(gz == GZ - 1)
    def _():
        ext[W : W + NY, W + NZ :] = jnp.zeros((NY, W, 4, LANES), f32)

    rows(NY, lambda n: n + W, pack)
    rows(NY - 2, lambda n: n + 3, smooth)
    rows(NY - 4, lambda n: n + 3, own_row)

    wait(ext.at[0 : 2 * W], halo_y.at[1])

    @pl.when(gy == 0)
    def _():
        ext[0:W] = jnp.zeros((W, NZ + 2 * W, 4, LANES), f32)

    @pl.when(gy == total_y - 1)
    def _():
        ext[W + NY :] = jnp.zeros((W, NZ + 2 * W, 4, LANES), f32)

    @pl.when(gz == 0)
    def _():
        for first in (0, W + NY):
            ext[first : first + W, 0:W] = jnp.zeros((W, W, 4, LANES), f32)

    @pl.when(gz == GZ - 1)
    def _():
        for first in (0, W + NY):
            ext[first : first + W, W + NZ :] = jnp.zeros((W, W, 4, LANES), f32)

    rows(2 * W, lambda n: n + NY * (n // 3), pack)
    rows(6, lambda n: n + 6 * (n // 3), smooth)
    row_work(0, False, keep(gy == 0))
    row_work(NY + 1, False, keep(gy == total_y - 1))
    rows(4, lambda n: n + 1 + 4 * (n // 2), own_row)

    def reduce(first, link, right, save):
        a, b, d, f, g = jnp.zeros_like(first), first, jnp.ones_like(first), jnp.zeros_like(first), right(0)
        for s in range(1, 8):
            c = link(s)
            inv = 1.0 / (b + c + d)
            t, w = b * inv, c * inv
            save[s - 1, 0], save[s - 1, 1], save[s - 1, 2] = g * inv, t, w
            a, f = a + t * d, f + t * g
            b, d, g = t * c, 1.0 + w * d, right(s) + w * g
        return a, b, d, f, g

    def explicit(s):
        now = base[s] + (RATE * 0.25) * (hy[s + 2] - hy[s])
        base[s] = now
        return now

    first_y = TAU * (cy[0] + cy[1]) * keep(gy == 0)
    port = reduce(first_y, lambda s: TAU * (cy[s] + cy[s + 1]), explicit, sav_y)
    for c, part in enumerate(port):
        for k in range(HZ):
            out_y[4 * k : 4 * k + 4, c] = part[k, 0:4]
            out_y[4 * (k + HZ) : 4 * (k + HZ) + 4, c] = part[k, 4:8]

    mine, i8, r8 = place * 4 + group, gy // 8, gy % 8
    pl.semaphore_wait(known, GROUPS - 1)
    for e, d in line:
        send(out_y.at[places[d] * 4 + groups[e]], in_y.at[i8, r8], sem_y, at(e, d))
    keep_own(out_y.at[mine], in_y.at[i8, r8], sem_y)

    first_z = TAU * (cz[:, 0] + cz[:, 1]) * low_in
    port = reduce(first_z, lambda s: TAU * (cz[:, s] + cz[:, s + 1]), lambda s: base[:, s], sav_z)
    for c, part in enumerate(port):
        out_z[:, c] = part
    for d in range(1, GZ):
        send(out_z.at[gzs[d]], in_z.at[gz], sem_z, (gy, gzs[d]))
    keep_own(out_z.at[gz], in_z.at[gz], sem_z)

    wait(in_z, sem_z.at[1])
    blocks = [tuple(in_z[k // 2, c, 4 * (k % 2) : 4 * (k % 2) + 4] for c in range(5)) for k in range(2 * GZ)]
    whole, z_steps = chain(blocks)
    u = whole[4] / (whole[1] + whole[2])
    sep_z[0] = jnp.zeros((4, LANES), f32)
    sep_z[2 * GZ] = u
    for k in reversed(range(2 * GZ - 1)):
        h, _, w = z_steps[k]
        u = h + w * u
        sep_z[k + 1] = u
    for d in range(1, GZ):
        send(sep_z.at[pl.ds(2 * gzs[d], 3)], back_z.at[gz], sem_bz, (gy, gzs[d]))
    keep_own(sep_z.at[pl.ds(2 * gz, 3)], back_z.at[gz], sem_bz)

    wait(in_y, sem_y.at[1])
    total, steps = chain([tuple(in_y[:, i, c] for c in range(5)) for i in range(8)])
    whole, run_steps = chain([tuple(part[s : s + 1] for part in total) for s in range(8)])
    u = whole[4] / (whole[1] + whole[2])
    ends = [u]
    for h, _, w in reversed(run_steps):
        u = h + w * u
        ends.insert(0, u)
    before = jnp.concatenate([jnp.zeros((1, LANES), f32)] + ends[:-1], axis=0)
    u = jnp.concatenate(ends, axis=0)
    out_b[:, 0, 0] = before
    out_b[:, 7, 1] = u
    for i in reversed(range(7)):
        h, t, w = steps[i]
        u = h + t * before + w * u
        out_b[:, i, 1] = u
        out_b[:, i + 1, 0] = u
    halves = [(p // 8, p % 8) for p in places]
    for e, d in line:
        send(out_b.at[2 * groups[e] + halves[d][0], halves[d][1]], back_y.at[mine], sem_by, at(e, d))
    keep_own(out_b.at[i8, r8], back_y.at[mine], sem_by)

    wait(back_z, sem_bz.at[1])
    before = jnp.concatenate([back_z[:, 0], back_z[:, 1]], axis=1)
    u = jnp.concatenate([back_z[:, 1], back_z[:, 2]], axis=1)
    base[:, HZ - 1] = u
    for s in reversed(range(HZ - 1)):
        u = sav_z[s, 0] + sav_z[s, 1] * before + sav_z[s, 2] * u
        base[:, s] = u

    wait(ext.at[W : W + NY, 0 : 2 * W], halo_z.at[0])
    wait(ext.at[0 : 2 * W], halo_y.at[0])
    wait(out_z.at[1:], sem_z.at[0])
    wait(back_z.at[1:], sem_bz.at[0])
    wait(out_y.at[1:], sem_y.at[0])
    wait(back_y.at[1:], sem_by.at[0])

    wait(back_y, sem_by.at[1])

    def both_halves(c):
        parts = [back_y[4 * k : 4 * k + 4, c] for k in range(NZ)]
        return jnp.stack([jnp.concatenate([parts[k], parts[k + HZ]], axis=0) for k in range(HZ)])

    before, u = both_halves(0), both_halves(1)
    for s in reversed(range(NY)):
        if s < NY - 1:
            u = sav_y[s, 0] + sav_y[s, 1] * before + sav_y[s, 2] * u
        both = 0.5 * (u + base[s])
        out[s, 0:HZ] = both[:, 0:4]
        out[s, HZ:] = both[:, 4:8]


def per_device(volume):
    vm = lambda *shape: pltpu.VMEM(shape, f32)
    full = (8, LANES)
    part = (4, LANES)
    result = pl.pallas_call(
        kernel,
        out_shape=jax.ShapeDtypeStruct((NY, NZ) + part, f32),
        in_specs=[pl.BlockSpec(memory_space=pl.ANY)],
        out_specs=pl.BlockSpec(memory_space=pltpu.VMEM),
        scratch_shapes=[
            vm(NY + 2 * W, NZ + 2 * W, *part),
            vm(NY + 2 * W, HZ + 2 * W, *full),
            vm(2, NY + 4, HZ + 4, *full),
            vm(NY + 2, HZ, *full),
            vm(NY, HZ + 1, *full),
            vm(NY + 2, HZ, *full),
            vm(NY, HZ, *full),
            vm(NY - 1, 3, HZ, *full),
            vm(HZ - 1, 3, NY, *full),
            vm(GROUP * GROUPS, 5, LANES),
            vm(8, 8, 5, LANES),
            vm(GZ, 5, *full),
            vm(GZ, 5, *full),
            vm(8, 8, 2, LANES),
            vm(2 * GZ + 1, *part),
            vm(GROUP * GROUPS, 2, LANES),
            vm(GZ, 3, *part),
            pltpu.SemaphoreType.DMA,
            pltpu.SemaphoreType.REGULAR,
        ]
        + [pltpu.SemaphoreType.DMA((2,)) for _ in range(6)],
        compiler_params=pltpu.CompilerParams(
            collective_id=0, has_side_effects=True, vmem_limit_bytes=32 * 1024 * 1024
        ),
        name="diffusion_step",
    )(volume)
    return result.reshape(volume.shape)


def solution(mesh):
    placed = P("gy", "gz", None)
    return jax.shard_map(
        per_device, mesh=mesh, in_specs=(placed,), out_specs=placed, check_vma=False
    )
```

```python
import functools

import jax
import jax.numpy as jnp
from jax import lax
from jax.experimental import pallas as pl
from jax.experimental.pallas import tpu as pltpu
from jax.sharding import PartitionSpec as P

TAU = 1024.0
CONTRAST = 0.05
RATE = 0.25

NY, NZ = 8, 16
HZ = NZ // 2
W = 3
GROUP = 16
GROUPS = 4
GZ = 8
LANES = 128
MESH = pl.DeviceIdType.MESH
f32 = jnp.float32


def lane_of(v):
    return lax.broadcasted_iota(jnp.int32, v.shape, v.ndim - 1)


def piece_of(v):
    return lax.broadcasted_iota(jnp.int32, v.shape, v.ndim - 2) % 4


def x_next(v, beyond=0.0):
    r = pltpu.roll(v, LANES - 1, v.ndim - 1)
    s = pltpu.roll(r, 7, v.ndim - 2)
    s = jnp.where(piece_of(v) == 3, beyond, s)
    return jnp.where(lane_of(v) == LANES - 1, s, r)


def x_prev(v, beyond=0.0):
    r = pltpu.roll(v, 1, v.ndim - 1)
    s = pltpu.roll(r, 1, v.ndim - 2)
    s = jnp.where(piece_of(v) == 0, beyond, s)
    return jnp.where(lane_of(v) == 0, s, r)


def join(block, after):
    a, b, d, f, g = block
    a2, b2, d2, f2, g2 = after
    m = d + a2
    inv = 1.0 / (b + b2 + m)
    t, w, h = b * inv, b2 * inv, g + f2
    return (a + t * m, t * b2, d2 + w * m, f + t * h, g2 + w * h), (h * inv, t, w)


def chain(blocks):
    total, steps = blocks[0], []
    for block in blocks[1:]:
        total, step = join(total, block)
        steps.append(step)
    return total, steps


def kernel(
    vol,
    out,
    ext,
    vp,
    sm,
    cy,
    cz,
    hy,
    base,
    sav_y,
    sav_z,
    out_y,
    in_y,
    out_z,
    in_z,
    out_b,
    sep_z,
    back_y,
    back_z,
    own_sem,
    ringed,
    known,
    halo_y,
    halo_z,
    sem_y,
    sem_z,
    sem_by,
    sem_bz,
):
    gy, gz = lax.axis_index("gy"), lax.axis_index("gz")
    total_y = GROUP * GROUPS
    group, place = gy // GROUP, gy % GROUP

    around = [(0, -1), (0, 1), (-1, -1), (-1, 1), (1, -1), (1, 1), (-1, 0), (1, 0)]
    ring = [8, 7, 9, 6, 10, 5, 11, 4, 12, 3, 13, 2, 14, 1, 15]
    line = [(e, d) for d in ring + [0] for e in (2, 1, 3, 0) if (e, d) != (0, 0)]

    def wrapped(x, n):
        return jnp.where(x >= n, x - n, x)

    places = [wrapped(place + d, GROUP) for d in range(GROUP)]
    groups = [wrapped(group + e, GROUPS) for e in range(GROUPS)]
    gzs = [wrapped(gz + d, GZ) for d in range(GZ)]
    gys = [gy, wrapped(gy + 1, total_y), wrapped(gy + total_y - 1, total_y)]

    def at(e, d):
        return (groups[e] * GROUP + places[d], gz)

    def send(src, dst, sems, peer):
        pltpu.make_async_remote_copy(
            src_ref=src,
            dst_ref=dst,
            send_sem=sems.at[0],
            recv_sem=sems.at[1],
            device_id=peer,
            device_id_type=MESH,
        ).start()

    def keep_own(src, dst, sems):
        pltpu.make_async_copy(src, dst, sems.at[1]).start()

    def wait(ref, sem):
        pltpu.make_async_copy(ref, ref, sem).wait()

    for t in range(4):
        pltpu.make_async_copy(
            vol.at[:, :, t * LANES : (t + 1) * LANES], ext.at[W : W + NY, W : W + NZ, t], own_sem
        ).start()

    barrier = pltpu.get_barrier_semaphore()
    peers = [(gys[i], gzs[j]) for i, j in around if i != 0]
    peers += [at(0, d % GROUP) for d in (4, -4, 3, -3, 2, -2, 1, -1)]
    peers += [(gy, gzs[d]) for d in range(1, GZ)]
    peers += [at(e, 0) for e in range(1, GROUPS)]
    for peer in peers:
        pl.semaphore_signal(barrier, inc=1, device_id=peer, device_id_type=MESH)
    wait(ext.at[W : W + NY, W : W + NZ], own_sem)
    pl.semaphore_wait(barrier, len(peers))

    def src_range(i, n):
        return slice(n, n + W) if i > 0 else slice(W, 2 * W) if i < 0 else slice(W, W + n)

    def dst_range(i, n):
        return slice(0, W) if i > 0 else slice(W + n, n + 2 * W) if i < 0 else slice(W, W + n)

    for i, j in around:
        send(
            ext.at[src_range(i, NY), src_range(j, NZ)],
            ext.at[dst_range(i, NY), dst_range(j, NZ)],
            halo_z if i == 0 else halo_y,
            (gys[i], gzs[j]),
        )
    for d in (4, GROUP - 4):
        pl.semaphore_signal(ringed, inc=1, device_id=at(0, d), device_id_type=MESH)

    def pack(r):
        row = ext[r]
        vp[r] = jnp.concatenate([row[: HZ + 2 * W], row[HZ:]], axis=1)

    def smooth(r):
        v = vp[r] + 2.0 * vp[r + 1] + vp[r + 2]
        v = v[:-2] + 2.0 * v[1:-1] + v[2:]
        sm[0, r] = v
        sm[1, r] = x_prev(v) + 2.0 * v + x_next(v)

    half = lax.broadcasted_iota(jnp.int32, (1, 8, LANES), 1) // 4
    low_in = jnp.where((half == 0) & (gz == 0), 0.0, 1.0).astype(f32)
    high_in = jnp.where((half == 1) & (gz == GZ - 1), 0.0, 1.0).astype(f32)

    def row_work(r, own_row, inside):
        mid = sm[1, r + 1]
        g_y = (sm[1, r + 2] - sm[1, r])[1:-1]
        g_z = mid[2:] - mid[:-2]
        core, filt = mid[1:-1], sm[0, r + 1][1:-1]
        g_x = x_next(core, filt) - x_prev(core, filt)
        yy, zz, xx = g_y * g_y, g_z * g_z, g_x * g_x
        small = f32(CONTRAST * 128.0 * 128.0)
        weight = 1.0 / (yy + zz + xx + small)
        off = weight
        if inside is not None:
            off = off * inside
        off = jnp.concatenate([off[:1] * low_in, off[1:-1], off[-1:] * high_in], axis=0)
        cy[r] = ((zz + xx + small) * weight)[1:-1]
        t_yz, t_xy = -off * g_y * g_z, -off * g_x * g_y
        v = vp[r + 2][2:-2]
        v_n = x_next(v)
        d_x = v_n - x_prev(v)
        v_z = vp[r + 2]
        d_z = (v_z[4:-2] - v_z[2:-4])
        hy[r] = t_xy[1:-1] * d_x[1:-1] + t_yz[1:-1] * d_z
        if own_row:
            t_xz = -off * g_x * g_z
            cz[r - 1] = ((yy + xx + small) * weight)[:-1]
            d_y = vp[r + 3][2:-2] - vp[r + 1][2:-2]
            k = t_xz * d_x + t_yz * d_y
            j = t_xy[1:-1] * d_y[1:-1] + t_xz[1:-1] * d_z
            t_xx = ((yy + zz + small) * weight)[1:-1]
            vc = v[1:-1]
            flux = 0.5 * (t_xx + x_next(t_xx)) * (v_n[1:-1] - vc)
            last = (lane_of(flux) == LANES - 1) & (piece_of(flux) == 3)
            flux = jnp.where(last, 0.0, flux)
            j = 0.25 * j
            change = (flux + x_next(j)) - x_prev(flux + j) + 0.25 * (k[2:] - k[:-2])
            base[r - 1] = vc + RATE * change

    def keep(cond):
        return jnp.where(cond, 0.0, 1.0).astype(f32)

    def rows(count, row, work):
        def body(n, carry):
            work(row(n))
            return carry

        lax.fori_loop(0, count, body, 0)

    def own_row(r):
        row_work(r, True, None)

    wait(ext.at[W : W + NY, 0 : 2 * W], halo_z.at[1])

    @pl.when(gz == 0)
    def _():
        ext[W : W + NY, 0:W] = jnp.zeros((NY, W, 4, LANES), f32)

    @pl.when(gz == GZ - 1)
    def _():
        ext[W : W + NY, W + NZ :] = jnp.zeros((NY, W, 4, LANES), f32)

    rows(NY, lambda n: n + W, pack)
    rows(NY - 2, lambda n: n + 3, smooth)
    rows(NY - 4, lambda n: n + 3, own_row)

    pl.semaphore_wait(ringed, 2)
    for e in range(1, GROUPS):
        pl.semaphore_signal(known, inc=1, device_id=at(e, 0), device_id_type=MESH)

    wait(ext.at[0 : 2 * W], halo_y.at[1])

    @pl.when(gy == 0)
    def _():
        ext[0:W] = jnp.zeros((W, NZ + 2 * W, 4, LANES), f32)

    @pl.when(gy == total_y - 1)
    def _():
        ext[W + NY :] = jnp.zeros((W, NZ + 2 * W, 4, LANES), f32)

    @pl.when(gz == 0)
    def _():
        for first in (0, W + NY):
            ext[first : first + W, 0:W] = jnp.zeros((W, W, 4, LANES), f32)

    @pl.when(gz == GZ - 1)
    def _():
        for first in (0, W + NY):
            ext[first : first + W, W + NZ :] = jnp.zeros((W, W, 4, LANES), f32)

    rows(2 * W, lambda n: n + NY * (n // 3), pack)
    rows(6, lambda n: n + 6 * (n // 3), smooth)
    row_work(0, False, keep(gy == 0))
    row_work(NY + 1, False, keep(gy == total_y - 1))
    rows(4, lambda n: n + 1 + 4 * (n // 2), own_row)

    def reduce(first, link, right, save):
        a, b, d, f, g = jnp.zeros_like(first), first, jnp.ones_like(first), jnp.zeros_like(first), right(0)
        for s in range(1, 8):
            c = link(s)
            inv = 1.0 / (b + c + d)
            t, w = b * inv, c * inv
            save[s - 1, 0], save[s - 1, 1], save[s - 1, 2] = g * inv, t, w
            a, f = a + t * d, f + t * g
            b, d, g = t * c, 1.0 + w * d, right(s) + w * g
        return a, b, d, f, g

    def explicit(s):
        now = base[s] + (RATE * 0.25) * (hy[s + 2] - hy[s])
        base[s] = now
        return now

    first_y = TAU * (cy[0] + cy[1]) * keep(gy == 0)
    port = reduce(first_y, lambda s: TAU * (cy[s] + cy[s + 1]), explicit, sav_y)
    for c, part in enumerate(port):
        for k in range(HZ):
            out_y[4 * k : 4 * k + 4, c] = part[k, 0:4]
            out_y[4 * (k + HZ) : 4 * (k + HZ) + 4, c] = part[k, 4:8]

    mine, i8, r8 = place * 4 + group, gy // 8, gy % 8
    pl.semaphore_wait(known, GROUPS - 1)
    for e, d in line:
        send(out_y.at[places[d] * 4 + groups[e]], in_y.at[i8, r8], sem_y, at(e, d))
    keep_own(out_y.at[mine], in_y.at[i8, r8], sem_y)

    first_z = TAU * (cz[:, 0] + cz[:, 1]) * low_in
    port = reduce(first_z, lambda s: TAU * (cz[:, s] + cz[:, s + 1]), lambda s: base[:, s], sav_z)
    for c, part in enumerate(port):
        out_z[:, c] = part
    for d in range(1, GZ):
        send(out_z.at[gzs[d]], in_z.at[gz], sem_z, (gy, gzs[d]))
    keep_own(out_z.at[gz], in_z.at[gz], sem_z)

    wait(in_z, sem_z.at[1])
    blocks = [tuple(in_z[k // 2, c, 4 * (k % 2) : 4 * (k % 2) + 4] for c in range(5)) for k in range(2 * GZ)]
    whole, z_steps = chain(blocks)
    u = whole[4] / (whole[1] + whole[2])
    sep_z[0] = jnp.zeros((4, LANES), f32)
    sep_z[2 * GZ] = u
    for k in reversed(range(2 * GZ - 1)):
        h, _, w = z_steps[k]
        u = h + w * u
        sep_z[k + 1] = u
    for d in range(1, GZ):
        send(sep_z.at[pl.ds(2 * gzs[d], 3)], back_z.at[gz], sem_bz, (gy, gzs[d]))
    keep_own(sep_z.at[pl.ds(2 * gz, 3)], back_z.at[gz], sem_bz)

    wait(in_y, sem_y.at[1])
    total, steps = chain([tuple(in_y[:, i, c] for c in range(5)) for i in range(8)])
    whole, run_steps = chain([tuple(part[s : s + 1] for part in total) for s in range(8)])
    u = whole[4] / (whole[1] + whole[2])
    ends = [u]
    for h, _, w in reversed(run_steps):
        u = h + w * u
        ends.insert(0, u)
    before = jnp.concatenate([jnp.zeros((1, LANES), f32)] + ends[:-1], axis=0)
    u = jnp.concatenate(ends, axis=0)
    out_b[:, 0, 0] = before
    out_b[:, 7, 1] = u
    for i in reversed(range(7)):
        h, t, w = steps[i]
        u = h + t * before + w * u
        out_b[:, i, 1] = u
        out_b[:, i + 1, 0] = u
    halves = [(p // 8, p % 8) for p in places]
    for e, d in line:
        send(out_b.at[2 * groups[e] + halves[d][0], halves[d][1]], back_y.at[mine], sem_by, at(e, d))
    keep_own(out_b.at[i8, r8], back_y.at[mine], sem_by)

    wait(back_z, sem_bz.at[1])
    before = jnp.concatenate([back_z[:, 0], back_z[:, 1]], axis=1)
    u = jnp.concatenate([back_z[:, 1], back_z[:, 2]], axis=1)
    base[:, HZ - 1] = u
    for s in reversed(range(HZ - 1)):
        u = sav_z[s, 0] + sav_z[s, 1] * before + sav_z[s, 2] * u
        base[:, s] = u

    wait(ext.at[W : W + NY, 0 : 2 * W], halo_z.at[0])
    wait(ext.at[0 : 2 * W], halo_y.at[0])
    wait(out_z.at[1:], sem_z.at[0])
    wait(back_z.at[1:], sem_bz.at[0])
    wait(out_y.at[1:], sem_y.at[0])
    wait(back_y.at[1:], sem_by.at[0])

    wait(back_y, sem_by.at[1])

    def both_halves(c):
        parts = [back_y[4 * k : 4 * k + 4, c] for k in range(NZ)]
        return jnp.stack([jnp.concatenate([parts[k], parts[k + HZ]], axis=0) for k in range(HZ)])

    before, u = both_halves(0), both_halves(1)
    for s in reversed(range(NY)):
        if s < NY - 1:
            u = sav_y[s, 0] + sav_y[s, 1] * before + sav_y[s, 2] * u
        both = 0.5 * (u + base[s])
        out[s, 0:HZ] = both[:, 0:4]
        out[s, HZ:] = both[:, 4:8]


def per_device(volume):
    vm = lambda *shape: pltpu.VMEM(shape, f32)
    full = (8, LANES)
    part = (4, LANES)
    result = pl.pallas_call(
        kernel,
        out_shape=jax.ShapeDtypeStruct((NY, NZ) + part, f32),
        in_specs=[pl.BlockSpec(memory_space=pl.ANY)],
        out_specs=pl.BlockSpec(memory_space=pltpu.VMEM),
        scratch_shapes=[
            vm(NY + 2 * W, NZ + 2 * W, *part),
            vm(NY + 2 * W, HZ + 2 * W, *full),
            vm(2, NY + 4, HZ + 4, *full),
            vm(NY + 2, HZ, *full),
            vm(NY, HZ + 1, *full),
            vm(NY + 2, HZ, *full),
            vm(NY, HZ, *full),
            vm(NY - 1, 3, HZ, *full),
            vm(HZ - 1, 3, NY, *full),
            vm(GROUP * GROUPS, 5, LANES),
            vm(8, 8, 5, LANES),
            vm(GZ, 5, *full),
            vm(GZ, 5, *full),
            vm(8, 8, 2, LANES),
            vm(2 * GZ + 1, *part),
            vm(GROUP * GROUPS, 2, LANES),
            vm(GZ, 3, *part),
            pltpu.SemaphoreType.DMA,
            pltpu.SemaphoreType.REGULAR,
            pltpu.SemaphoreType.REGULAR,
        ]
        + [pltpu.SemaphoreType.DMA((2,)) for _ in range(6)],
        compiler_params=pltpu.CompilerParams(
            collective_id=0, has_side_effects=True, vmem_limit_bytes=32 * 1024 * 1024
        ),
        name="diffusion_step",
    )(volume)
    return result.reshape(volume.shape)


def solution(mesh):
    placed = P("gy", "gz", None)
    return jax.shard_map(
        per_device, mesh=mesh, in_specs=(placed,), out_specs=placed, check_vma=False
    )
```

```python
import functools

import jax
import jax.numpy as jnp
from jax import lax
from jax.experimental import pallas as pl
from jax.experimental.pallas import tpu as pltpu
from jax.sharding import PartitionSpec as P

TAU = 1024.0
CONTRAST = 0.05
RATE = 0.25

NY, NZ = 8, 16
HZ = NZ // 2
W = 3
GROUP = 16
GROUPS = 4
GZ = 8
LANES = 128
MESH = pl.DeviceIdType.MESH
f32 = jnp.float32


def lane_of(v):
    return lax.broadcasted_iota(jnp.int32, v.shape, v.ndim - 1)


def piece_of(v):
    return lax.broadcasted_iota(jnp.int32, v.shape, v.ndim - 2) % 4


def x_next(v, beyond=0.0):
    r = pltpu.roll(v, LANES - 1, v.ndim - 1)
    s = pltpu.roll(r, 7, v.ndim - 2)
    s = jnp.where(piece_of(v) == 3, beyond, s)
    return jnp.where(lane_of(v) == LANES - 1, s, r)


def x_prev(v, beyond=0.0):
    r = pltpu.roll(v, 1, v.ndim - 1)
    s = pltpu.roll(r, 1, v.ndim - 2)
    s = jnp.where(piece_of(v) == 0, beyond, s)
    return jnp.where(lane_of(v) == 0, s, r)


def join(block, after):
    a, b, d, f, g = block
    a2, b2, d2, f2, g2 = after
    m = d + a2
    inv = 1.0 / (b + b2 + m)
    t, w, h = b * inv, b2 * inv, g + f2
    return (a + t * m, t * b2, d2 + w * m, f + t * h, g2 + w * h), (h * inv, t, w)


def chain(blocks):
    total, steps = blocks[0], []
    for block in blocks[1:]:
        total, step = join(total, block)
        steps.append(step)
    return total, steps


def kernel(
    vol,
    out,
    ext,
    vp,
    sm,
    cy,
    cz,
    hy,
    base,
    sav_y,
    sav_z,
    out_y,
    in_y,
    out_z,
    in_z,
    out_b,
    sep_z,
    back_y,
    back_z,
    own_sem,
    ringed,
    known,
    halo_y,
    halo_z,
    sem_y,
    sem_z,
    sem_by,
    sem_bz,
):
    gy, gz = lax.axis_index("gy"), lax.axis_index("gz")
    total_y = GROUP * GROUPS
    group, place = gy // GROUP, gy % GROUP

    around = [(0, -1), (0, 1), (-1, -1), (-1, 1), (1, -1), (1, 1), (-1, 0), (1, 0)]
    ring = [8, 7, 9, 6, 10, 5, 11, 4, 12, 3, 13, 2, 14, 1, 15]
    line = [(e, d) for d in ring + [0] for e in (2, 1, 3, 0) if (e, d) != (0, 0)]

    def wrapped(x, n):
        return jnp.where(x >= n, x - n, x)

    places = [wrapped(place + d, GROUP) for d in range(GROUP)]
    groups = [wrapped(group + e, GROUPS) for e in range(GROUPS)]
    gzs = [wrapped(gz + d, GZ) for d in range(GZ)]
    gys = [gy, wrapped(gy + 1, total_y), wrapped(gy + total_y - 1, total_y)]

    def at(e, d):
        return (groups[e] * GROUP + places[d], gz)

    def send(src, dst, sems, peer):
        pltpu.make_async_remote_copy(
            src_ref=src,
            dst_ref=dst,
            send_sem=sems.at[0],
            recv_sem=sems.at[1],
            device_id=peer,
            device_id_type=MESH,
        ).start()

    def keep_own(src, dst, sems):
        pltpu.make_async_copy(src, dst, sems.at[1]).start()

    def wait(ref, sem):
        pltpu.make_async_copy(ref, ref, sem).wait()

    for t in range(4):
        pltpu.make_async_copy(
            vol.at[:, :, t * LANES : (t + 1) * LANES], ext.at[W : W + NY, W : W + NZ, t], own_sem
        ).start()

    barrier = pltpu.get_barrier_semaphore()
    peers = [(gys[i], gzs[j]) for i, j in around if i != 0]
    peers += [at(0, d % GROUP) for d in (4, -4, 3, -3, 2, -2, 1, -1)]
    peers += [(gy, gzs[d]) for d in range(1, GZ)]
    peers += [at(e, 0) for e in range(1, GROUPS)]
    for peer in peers:
        pl.semaphore_signal(barrier, inc=1, device_id=peer, device_id_type=MESH)
    wait(ext.at[W : W + NY, W : W + NZ], own_sem)
    pl.semaphore_wait(barrier, len(peers))

    def src_range(i, n):
        return slice(n, n + W) if i > 0 else slice(W, 2 * W) if i < 0 else slice(W, W + n)

    def dst_range(i, n):
        return slice(0, W) if i > 0 else slice(W + n, n + 2 * W) if i < 0 else slice(W, W + n)

    for i, j in around:
        send(
            ext.at[src_range(i, NY), src_range(j, NZ)],
            ext.at[dst_range(i, NY), dst_range(j, NZ)],
            halo_z if i == 0 else halo_y,
            (gys[i], gzs[j]),
        )
    for d in (4, GROUP - 4):
        pl.semaphore_signal(ringed, inc=1, device_id=at(0, d), device_id_type=MESH)

    def pack(r):
        row = ext[r]
        vp[r] = jnp.concatenate([row[: HZ + 2 * W], row[HZ:]], axis=1)

    def smooth(r):
        v = vp[r] + 2.0 * vp[r + 1] + vp[r + 2]
        v = v[:-2] + 2.0 * v[1:-1] + v[2:]
        sm[0, r] = v
        sm[1, r] = x_prev(v) + 2.0 * v + x_next(v)

    half = lax.broadcasted_iota(jnp.int32, (1, 8, LANES), 1) // 4
    low_in = jnp.where((half == 0) & (gz == 0), 0.0, 1.0).astype(f32)
    high_in = jnp.where((half == 1) & (gz == GZ - 1), 0.0, 1.0).astype(f32)

    def row_work(r, own_row, inside):
        mid = sm[1, r + 1]
        g_y = (sm[1, r + 2] - sm[1, r])[1:-1]
        g_z = mid[2:] - mid[:-2]
        core, filt = mid[1:-1], sm[0, r + 1][1:-1]
        g_x = x_next(core, filt) - x_prev(core, filt)
        yy, zz, xx = g_y * g_y, g_z * g_z, g_x * g_x
        small = f32(CONTRAST * 128.0 * 128.0)
        weight = 1.0 / (yy + zz + xx + small)
        off = weight
        if inside is not None:
            off = off * inside
        off = jnp.concatenate([off[:1] * low_in, off[1:-1], off[-1:] * high_in], axis=0)
        cy[r] = ((zz + xx + small) * weight)[1:-1]
        t_yz, t_xy = -off * g_y * g_z, -off * g_x * g_y
        v = vp[r + 2][2:-2]
        v_n = x_next(v)
        d_x = v_n - x_prev(v)
        v_z = vp[r + 2]
        d_z = (v_z[4:-2] - v_z[2:-4])
        hy[r] = t_xy[1:-1] * d_x[1:-1] + t_yz[1:-1] * d_z
        if own_row:
            t_xz = -off * g_x * g_z
            cz[r - 1] = ((yy + xx + small) * weight)[:-1]
            d_y = vp[r + 3][2:-2] - vp[r + 1][2:-2]
            k = t_xz * d_x + t_yz * d_y
            j = t_xy[1:-1] * d_y[1:-1] + t_xz[1:-1] * d_z
            t_xx = ((yy + zz + small) * weight)[1:-1]
            vc = v[1:-1]
            flux = 0.5 * (t_xx + x_next(t_xx)) * (v_n[1:-1] - vc)
            last = (lane_of(flux) == LANES - 1) & (piece_of(flux) == 3)
            flux = jnp.where(last, 0.0, flux)
            j = 0.25 * j
            change = (flux + x_next(j)) - x_prev(flux + j) + 0.25 * (k[2:] - k[:-2])
            base[r - 1] = vc + RATE * change

    def keep(cond):
        return jnp.where(cond, 0.0, 1.0).astype(f32)

    def rows(count, row, work):
        def body(n, carry):
            work(row(n))
            return carry

        lax.fori_loop(0, count, body, 0, unroll=4 if count % 4 == 0 else 2)

    def own_row(r):
        row_work(r, True, None)

    wait(ext.at[W : W + NY, 0 : 2 * W], halo_z.at[1])

    @pl.when(gz == 0)
    def _():
        ext[W : W + NY, 0:W] = jnp.zeros((NY, W, 4, LANES), f32)

    @pl.when(gz == GZ - 1)
    def _():
        ext[W : W + NY, W + NZ :] = jnp.zeros((NY, W, 4, LANES), f32)

    rows(NY, lambda n: n + W, pack)
    rows(NY - 2, lambda n: n + 3, smooth)
    rows(NY - 4, lambda n: n + 3, own_row)

    pl.semaphore_wait(ringed, 2)
    for e in range(1, GROUPS):
        pl.semaphore_signal(known, inc=1, device_id=at(e, 0), device_id_type=MESH)

    wait(ext.at[0 : 2 * W], halo_y.at[1])

    @pl.when(gy == 0)
    def _():
        ext[0:W] = jnp.zeros((W, NZ + 2 * W, 4, LANES), f32)

    @pl.when(gy == total_y - 1)
    def _():
        ext[W + NY :] = jnp.zeros((W, NZ + 2 * W, 4, LANES), f32)

    @pl.when(gz == 0)
    def _():
        for first in (0, W + NY):
            ext[first : first + W, 0:W] = jnp.zeros((W, W, 4, LANES), f32)

    @pl.when(gz == GZ - 1)
    def _():
        for first in (0, W + NY):
            ext[first : first + W, W + NZ :] = jnp.zeros((W, W, 4, LANES), f32)

    rows(2 * W, lambda n: n + NY * (n // 3), pack)
    rows(6, lambda n: n + 6 * (n // 3), smooth)
    row_work(0, False, keep(gy == 0))
    row_work(NY + 1, False, keep(gy == total_y - 1))
    rows(4, lambda n: n + 1 + 4 * (n // 2), own_row)

    def reduce(first, link, right, save):
        a, b, d, f, g = jnp.zeros_like(first), first, jnp.ones_like(first), jnp.zeros_like(first), right(0)
        for s in range(1, 8):
            c = link(s)
            inv = 1.0 / (b + c + d)
            t, w = b * inv, c * inv
            save[s - 1, 0], save[s - 1, 1], save[s - 1, 2] = g * inv, t, w
            a, f = a + t * d, f + t * g
            b, d, g = t * c, 1.0 + w * d, right(s) + w * g
        return a, b, d, f, g

    def explicit(s):
        now = base[s] + (RATE * 0.25) * (hy[s + 2] - hy[s])
        base[s] = now
        return now

    first_y = TAU * (cy[0] + cy[1]) * keep(gy == 0)
    port = reduce(first_y, lambda s: TAU * (cy[s] + cy[s + 1]), explicit, sav_y)
    for c, part in enumerate(port):
        for k in range(HZ):
            out_y[4 * k : 4 * k + 4, c] = part[k, 0:4]
            out_y[4 * (k + HZ) : 4 * (k + HZ) + 4, c] = part[k, 4:8]

    mine, i8, r8 = place * 4 + group, gy // 8, gy % 8
    pl.semaphore_wait(known, GROUPS - 1)
    for e, d in line:
        send(out_y.at[places[d] * 4 + groups[e]], in_y.at[i8, r8], sem_y, at(e, d))
    keep_own(out_y.at[mine], in_y.at[i8, r8], sem_y)

    first_z = TAU * (cz[:, 0] + cz[:, 1]) * low_in
    port = reduce(first_z, lambda s: TAU * (cz[:, s] + cz[:, s + 1]), lambda s: base[:, s], sav_z)
    for c, part in enumerate(port):
        out_z[:, c] = part
    for d in range(1, GZ):
        send(out_z.at[gzs[d]], in_z.at[gz], sem_z, (gy, gzs[d]))
    keep_own(out_z.at[gz], in_z.at[gz], sem_z)

    wait(in_z, sem_z.at[1])
    blocks = [tuple(in_z[k // 2, c, 4 * (k % 2) : 4 * (k % 2) + 4] for c in range(5)) for k in range(2 * GZ)]
    whole, z_steps = chain(blocks)
    u = whole[4] / (whole[1] + whole[2])
    sep_z[0] = jnp.zeros((4, LANES), f32)
    sep_z[2 * GZ] = u
    for k in reversed(range(2 * GZ - 1)):
        h, _, w = z_steps[k]
        u = h + w * u
        sep_z[k + 1] = u
    for d in range(1, GZ):
        send(sep_z.at[pl.ds(2 * gzs[d], 3)], back_z.at[gz], sem_bz, (gy, gzs[d]))
    keep_own(sep_z.at[pl.ds(2 * gz, 3)], back_z.at[gz], sem_bz)

    wait(in_y, sem_y.at[1])
    total, steps = chain([tuple(in_y[:, i, c] for c in range(5)) for i in range(8)])
    whole, run_steps = chain([tuple(part[s : s + 1] for part in total) for s in range(8)])
    u = whole[4] / (whole[1] + whole[2])
    ends = [u]
    for h, _, w in reversed(run_steps):
        u = h + w * u
        ends.insert(0, u)
    before = jnp.concatenate([jnp.zeros((1, LANES), f32)] + ends[:-1], axis=0)
    u = jnp.concatenate(ends, axis=0)
    out_b[:, 0, 0] = before
    out_b[:, 7, 1] = u
    for i in reversed(range(7)):
        h, t, w = steps[i]
        u = h + t * before + w * u
        out_b[:, i, 1] = u
        out_b[:, i + 1, 0] = u
    halves = [(p // 8, p % 8) for p in places]
    for e, d in line:
        send(out_b.at[2 * groups[e] + halves[d][0], halves[d][1]], back_y.at[mine], sem_by, at(e, d))
    keep_own(out_b.at[i8, r8], back_y.at[mine], sem_by)

    wait(back_z, sem_bz.at[1])
    before = jnp.concatenate([back_z[:, 0], back_z[:, 1]], axis=1)
    u = jnp.concatenate([back_z[:, 1], back_z[:, 2]], axis=1)
    base[:, HZ - 1] = u
    for s in reversed(range(HZ - 1)):
        u = sav_z[s, 0] + sav_z[s, 1] * before + sav_z[s, 2] * u
        base[:, s] = u

    wait(ext.at[W : W + NY, 0 : 2 * W], halo_z.at[0])
    wait(ext.at[0 : 2 * W], halo_y.at[0])
    wait(out_z.at[1:], sem_z.at[0])
    wait(back_z.at[1:], sem_bz.at[0])
    wait(out_y.at[1:], sem_y.at[0])
    wait(back_y.at[1:], sem_by.at[0])

    wait(back_y, sem_by.at[1])

    def both_halves(c):
        parts = [back_y[4 * k : 4 * k + 4, c] for k in range(NZ)]
        return jnp.stack([jnp.concatenate([parts[k], parts[k + HZ]], axis=0) for k in range(HZ)])

    before, u = both_halves(0), both_halves(1)
    for s in reversed(range(NY)):
        if s < NY - 1:
            u = sav_y[s, 0] + sav_y[s, 1] * before + sav_y[s, 2] * u
        both = 0.5 * (u + base[s])
        out[s, 0:HZ] = both[:, 0:4]
        out[s, HZ:] = both[:, 4:8]


def per_device(volume):
    vm = lambda *shape: pltpu.VMEM(shape, f32)
    full = (8, LANES)
    part = (4, LANES)
    result = pl.pallas_call(
        kernel,
        out_shape=jax.ShapeDtypeStruct((NY, NZ) + part, f32),
        in_specs=[pl.BlockSpec(memory_space=pl.ANY)],
        out_specs=pl.BlockSpec(memory_space=pltpu.VMEM),
        scratch_shapes=[
            vm(NY + 2 * W, NZ + 2 * W, *part),
            vm(NY + 2 * W, HZ + 2 * W, *full),
            vm(2, NY + 4, HZ + 4, *full),
            vm(NY + 2, HZ, *full),
            vm(NY, HZ + 1, *full),
            vm(NY + 2, HZ, *full),
            vm(NY, HZ, *full),
            vm(NY - 1, 3, HZ, *full),
            vm(HZ - 1, 3, NY, *full),
            vm(GROUP * GROUPS, 5, LANES),
            vm(8, 8, 5, LANES),
            vm(GZ, 5, *full),
            vm(GZ, 5, *full),
            vm(8, 8, 2, LANES),
            vm(2 * GZ + 1, *part),
            vm(GROUP * GROUPS, 2, LANES),
            vm(GZ, 3, *part),
            pltpu.SemaphoreType.DMA,
            pltpu.SemaphoreType.REGULAR,
            pltpu.SemaphoreType.REGULAR,
        ]
        + [pltpu.SemaphoreType.DMA((2,)) for _ in range(6)],
        compiler_params=pltpu.CompilerParams(
            collective_id=0, has_side_effects=True, vmem_limit_bytes=32 * 1024 * 1024
        ),
        name="diffusion_step",
    )(volume)
    return result.reshape(volume.shape)


def solution(mesh):
    placed = P("gy", "gz", None)
    return jax.shard_map(
        per_device, mesh=mesh, in_specs=(placed,), out_specs=placed, check_vma=False
    )
```

```python
import functools

import jax
import jax.numpy as jnp
from jax import lax
from jax.experimental import pallas as pl
from jax.experimental.pallas import tpu as pltpu
from jax.sharding import PartitionSpec as P

TAU = 1024.0
CONTRAST = 0.05
RATE = 0.25

NY, NZ = 8, 16
HZ = NZ // 2
W = 3
GROUP = 16
GROUPS = 4
GZ = 8
LANES = 128
MESH = pl.DeviceIdType.MESH
f32 = jnp.float32


def lane_of(v):
    return lax.broadcasted_iota(jnp.int32, v.shape, v.ndim - 1)


def piece_of(v):
    return lax.broadcasted_iota(jnp.int32, v.shape, v.ndim - 2) % 4


def x_next(v, beyond=0.0):
    r = pltpu.roll(v, LANES - 1, v.ndim - 1)
    s = pltpu.roll(r, 7, v.ndim - 2)
    s = jnp.where(piece_of(v) == 3, beyond, s)
    return jnp.where(lane_of(v) == LANES - 1, s, r)


def x_prev(v, beyond=0.0):
    r = pltpu.roll(v, 1, v.ndim - 1)
    s = pltpu.roll(r, 1, v.ndim - 2)
    s = jnp.where(piece_of(v) == 0, beyond, s)
    return jnp.where(lane_of(v) == 0, s, r)


def join(block, after):
    a, b, d, f, g = block
    a2, b2, d2, f2, g2 = after
    m = d + a2
    inv = 1.0 / (b + b2 + m)
    t, w, h = b * inv, b2 * inv, g + f2
    return (a + t * m, t * b2, d2 + w * m, f + t * h, g2 + w * h), (h * inv, t, w)


def chain(blocks):
    total, steps = blocks[0], []
    for block in blocks[1:]:
        total, step = join(total, block)
        steps.append(step)
    return total, steps


def kernel(
    vol,
    out,
    ext,
    vp,
    sm,
    cy,
    cz,
    hy,
    base,
    sav_y,
    sav_z,
    out_y,
    in_y,
    out_z,
    in_z,
    out_b,
    sep_z,
    back_y,
    back_z,
    own_sem,
    ringed,
    known,
    halo_y,
    halo_z,
    sem_y,
    sem_z,
    sem_by,
    sem_bz,
):
    gy, gz = lax.axis_index("gy"), lax.axis_index("gz")
    total_y = GROUP * GROUPS
    group, place = gy // GROUP, gy % GROUP

    around = [(-1, -1), (-1, 1), (1, -1), (1, 1), (-1, 0), (1, 0), (0, -1), (0, 1)]
    ring = [8, 7, 9, 6, 10, 5, 11, 4, 12, 3, 13, 2, 14, 1, 15]
    line = [(e, d) for d in ring + [0] for e in (2, 1, 3, 0) if (e, d) != (0, 0)]

    def wrapped(x, n):
        return jnp.where(x >= n, x - n, x)

    places = [wrapped(place + d, GROUP) for d in range(GROUP)]
    groups = [wrapped(group + e, GROUPS) for e in range(GROUPS)]
    gzs = [wrapped(gz + d, GZ) for d in range(GZ)]
    gys = [gy, wrapped(gy + 1, total_y), wrapped(gy + total_y - 1, total_y)]

    def at(e, d):
        return (groups[e] * GROUP + places[d], gz)

    def send(src, dst, sems, peer):
        pltpu.make_async_remote_copy(
            src_ref=src,
            dst_ref=dst,
            send_sem=sems.at[0],
            recv_sem=sems.at[1],
            device_id=peer,
            device_id_type=MESH,
        ).start()

    def keep_own(src, dst, sems):
        pltpu.make_async_copy(src, dst, sems.at[1]).start()

    def wait(ref, sem):
        pltpu.make_async_copy(ref, ref, sem).wait()

    for t in range(4):
        pltpu.make_async_copy(
            vol.at[:, :, t * LANES : (t + 1) * LANES], ext.at[W : W + NY, W : W + NZ, t], own_sem
        ).start()

    barrier = pltpu.get_barrier_semaphore()
    peers = [(gys[i], gzs[j]) for i, j in around if i != 0]
    peers += [at(0, d % GROUP) for d in (4, -4, 3, -3, 2, -2, 1, -1)]
    peers += [(gy, gzs[d]) for d in range(1, GZ)]
    peers += [at(e, 0) for e in range(1, GROUPS)]
    for peer in peers:
        pl.semaphore_signal(barrier, inc=1, device_id=peer, device_id_type=MESH)
    wait(ext.at[W : W + NY, W : W + NZ], own_sem)
    pl.semaphore_wait(barrier, len(peers))

    def src_range(i, n):
        return slice(n, n + W) if i > 0 else slice(W, 2 * W) if i < 0 else slice(W, W + n)

    def dst_range(i, n):
        return slice(0, W) if i > 0 else slice(W + n, n + 2 * W) if i < 0 else slice(W, W + n)

    for i, j in around:
        send(
            ext.at[src_range(i, NY), src_range(j, NZ)],
            ext.at[dst_range(i, NY), dst_range(j, NZ)],
            halo_z if i == 0 else halo_y,
            (gys[i], gzs[j]),
        )
    for d in (4, GROUP - 4):
        pl.semaphore_signal(ringed, inc=1, device_id=at(0, d), device_id_type=MESH)

    def pack(r):
        row = ext[r]
        vp[r] = jnp.concatenate([row[: HZ + 2 * W], row[HZ:]], axis=1)

    def smooth(r):
        v = vp[r] + 2.0 * vp[r + 1] + vp[r + 2]
        v = v[:-2] + 2.0 * v[1:-1] + v[2:]
        sm[0, r] = v
        sm[1, r] = x_prev(v) + 2.0 * v + x_next(v)

    half = lax.broadcasted_iota(jnp.int32, (1, 8, LANES), 1) // 4
    low_in = jnp.where((half == 0) & (gz == 0), 0.0, 1.0).astype(f32)
    high_in = jnp.where((half == 1) & (gz == GZ - 1), 0.0, 1.0).astype(f32)

    def row_work(r, own_row, inside):
        mid = sm[1, r + 1]
        g_y = (sm[1, r + 2] - sm[1, r])[1:-1]
        g_z = mid[2:] - mid[:-2]
        core, filt = mid[1:-1], sm[0, r + 1][1:-1]
        g_x = x_next(core, filt) - x_prev(core, filt)
        yy, zz, xx = g_y * g_y, g_z * g_z, g_x * g_x
        small = f32(CONTRAST * 128.0 * 128.0)
        weight = 1.0 / (yy + zz + xx + small)
        off = weight
        if inside is not None:
            off = off * inside
        off = jnp.concatenate([off[:1] * low_in, off[1:-1], off[-1:] * high_in], axis=0)
        cy[r] = ((zz + xx + small) * weight)[1:-1]
        t_yz, t_xy = -off * g_y * g_z, -off * g_x * g_y
        v = vp[r + 2][2:-2]
        v_n = x_next(v)
        d_x = v_n - x_prev(v)
        v_z = vp[r + 2]
        d_z = (v_z[4:-2] - v_z[2:-4])
        hy[r] = t_xy[1:-1] * d_x[1:-1] + t_yz[1:-1] * d_z
        if own_row:
            t_xz = -off * g_x * g_z
            cz[r - 1] = ((yy + xx + small) * weight)[:-1]
            d_y = vp[r + 3][2:-2] - vp[r + 1][2:-2]
            k = t_xz * d_x + t_yz * d_y
            j = t_xy[1:-1] * d_y[1:-1] + t_xz[1:-1] * d_z
            t_xx = ((yy + zz + small) * weight)[1:-1]
            vc = v[1:-1]
            flux = 0.5 * (t_xx + x_next(t_xx)) * (v_n[1:-1] - vc)
            last = (lane_of(flux) == LANES - 1) & (piece_of(flux) == 3)
            flux = jnp.where(last, 0.0, flux)
            j = 0.25 * j
            change = (flux + x_next(j)) - x_prev(flux + j) + 0.25 * (k[2:] - k[:-2])
            base[r - 1] = vc + RATE * change

    def keep(cond):
        return jnp.where(cond, 0.0, 1.0).astype(f32)

    def rows(count, row, work):
        def body(n, carry):
            work(row(n))
            return carry

        lax.fori_loop(0, count, body, 0, unroll=4 if count % 4 == 0 else 2)

    def own_row(r):
        row_work(r, True, None)

    wait(ext.at[W : W + NY, 0 : 2 * W], halo_z.at[1])

    @pl.when(gz == 0)
    def _():
        ext[W : W + NY, 0:W] = jnp.zeros((NY, W, 4, LANES), f32)

    @pl.when(gz == GZ - 1)
    def _():
        ext[W : W + NY, W + NZ :] = jnp.zeros((NY, W, 4, LANES), f32)

    rows(NY, lambda n: n + W, pack)
    rows(NY - 2, lambda n: n + 3, smooth)
    rows(NY - 4, lambda n: n + 3, own_row)

    pl.semaphore_wait(ringed, 2)
    for e in range(1, GROUPS):
        pl.semaphore_signal(known, inc=1, device_id=at(e, 0), device_id_type=MESH)

    wait(ext.at[0 : 2 * W], halo_y.at[1])

    @pl.when(gy == 0)
    def _():
        ext[0:W] = jnp.zeros((W, NZ + 2 * W, 4, LANES), f32)

    @pl.when(gy == total_y - 1)
    def _():
        ext[W + NY :] = jnp.zeros((W, NZ + 2 * W, 4, LANES), f32)

    @pl.when(gz == 0)
    def _():
        for first in (0, W + NY):
            ext[first : first + W, 0:W] = jnp.zeros((W, W, 4, LANES), f32)

    @pl.when(gz == GZ - 1)
    def _():
        for first in (0, W + NY):
            ext[first : first + W, W + NZ :] = jnp.zeros((W, W, 4, LANES), f32)

    rows(2 * W, lambda n: n + NY * (n // 3), pack)
    rows(6, lambda n: n + 6 * (n // 3), smooth)
    row_work(0, False, keep(gy == 0))
    row_work(NY + 1, False, keep(gy == total_y - 1))
    rows(4, lambda n: n + 1 + 4 * (n // 2), own_row)

    def reduce(first, link, right, save):
        a, b, d, f, g = jnp.zeros_like(first), first, jnp.ones_like(first), jnp.zeros_like(first), right(0)
        for s in range(1, 8):
            c = link(s)
            inv = 1.0 / (b + c + d)
            t, w = b * inv, c * inv
            save[s - 1, 0], save[s - 1, 1], save[s - 1, 2] = g * inv, t, w
            a, f = a + t * d, f + t * g
            b, d, g = t * c, 1.0 + w * d, right(s) + w * g
        return a, b, d, f, g

    def explicit(s):
        now = base[s] + (RATE * 0.25) * (hy[s + 2] - hy[s])
        base[s] = now
        return now

    first_y = TAU * (cy[0] + cy[1]) * keep(gy == 0)
    port = reduce(first_y, lambda s: TAU * (cy[s] + cy[s + 1]), explicit, sav_y)
    for c, part in enumerate(port):
        for k in range(HZ):
            out_y[4 * k : 4 * k + 4, c] = part[k, 0:4]
            out_y[4 * (k + HZ) : 4 * (k + HZ) + 4, c] = part[k, 4:8]

    mine, i8, r8 = place * 4 + group, gy // 8, gy % 8
    pl.semaphore_wait(known, GROUPS - 1)
    for e, d in line:
        send(out_y.at[places[d] * 4 + groups[e]], in_y.at[i8, r8], sem_y, at(e, d))
    keep_own(out_y.at[mine], in_y.at[i8, r8], sem_y)

    first_z = TAU * (cz[:, 0] + cz[:, 1]) * low_in
    port = reduce(first_z, lambda s: TAU * (cz[:, s] + cz[:, s + 1]), lambda s: base[:, s], sav_z)
    for c, part in enumerate(port):
        out_z[:, c] = part
    for d in range(1, GZ):
        send(out_z.at[gzs[d]], in_z.at[gz], sem_z, (gy, gzs[d]))
    keep_own(out_z.at[gz], in_z.at[gz], sem_z)

    wait(in_z, sem_z.at[1])
    blocks = [tuple(in_z[k // 2, c, 4 * (k % 2) : 4 * (k % 2) + 4] for c in range(5)) for k in range(2 * GZ)]
    whole, z_steps = chain(blocks)
    u = whole[4] / (whole[1] + whole[2])
    sep_z[0] = jnp.zeros((4, LANES), f32)
    sep_z[2 * GZ] = u
    for k in reversed(range(2 * GZ - 1)):
        h, _, w = z_steps[k]
        u = h + w * u
        sep_z[k + 1] = u
    for d in range(1, GZ):
        send(sep_z.at[pl.ds(2 * gzs[d], 3)], back_z.at[gz], sem_bz, (gy, gzs[d]))
    keep_own(sep_z.at[pl.ds(2 * gz, 3)], back_z.at[gz], sem_bz)

    wait(in_y, sem_y.at[1])
    total, steps = chain([tuple(in_y[:, i, c] for c in range(5)) for i in range(8)])
    whole, run_steps = chain([tuple(part[s : s + 1] for part in total) for s in range(8)])
    u = whole[4] / (whole[1] + whole[2])
    ends = [u]
    for h, _, w in reversed(run_steps):
        u = h + w * u
        ends.insert(0, u)
    before = jnp.concatenate([jnp.zeros((1, LANES), f32)] + ends[:-1], axis=0)
    u = jnp.concatenate(ends, axis=0)
    out_b[:, 0, 0] = before
    out_b[:, 7, 1] = u
    for i in reversed(range(7)):
        h, t, w = steps[i]
        u = h + t * before + w * u
        out_b[:, i, 1] = u
        out_b[:, i + 1, 0] = u
    halves = [(p // 8, p % 8) for p in places]
    for e, d in line:
        send(out_b.at[2 * groups[e] + halves[d][0], halves[d][1]], back_y.at[mine], sem_by, at(e, d))
    keep_own(out_b.at[i8, r8], back_y.at[mine], sem_by)

    wait(back_z, sem_bz.at[1])
    before = jnp.concatenate([back_z[:, 0], back_z[:, 1]], axis=1)
    u = jnp.concatenate([back_z[:, 1], back_z[:, 2]], axis=1)
    base[:, HZ - 1] = u
    for s in reversed(range(HZ - 1)):
        u = sav_z[s, 0] + sav_z[s, 1] * before + sav_z[s, 2] * u
        base[:, s] = u

    wait(ext.at[W : W + NY, 0 : 2 * W], halo_z.at[0])
    wait(ext.at[0 : 2 * W], halo_y.at[0])
    wait(out_z.at[1:], sem_z.at[0])
    wait(back_z.at[1:], sem_bz.at[0])
    wait(out_y.at[1:], sem_y.at[0])
    wait(back_y.at[1:], sem_by.at[0])

    wait(back_y, sem_by.at[1])

    def both_halves(c):
        parts = [back_y[4 * k : 4 * k + 4, c] for k in range(NZ)]
        return jnp.stack([jnp.concatenate([parts[k], parts[k + HZ]], axis=0) for k in range(HZ)])

    before, u = both_halves(0), both_halves(1)
    for s in reversed(range(NY)):
        if s < NY - 1:
            u = sav_y[s, 0] + sav_y[s, 1] * before + sav_y[s, 2] * u
        both = 0.5 * (u + base[s])
        out[s, 0:HZ] = both[:, 0:4]
        out[s, HZ:] = both[:, 4:8]


def per_device(volume):
    vm = lambda *shape: pltpu.VMEM(shape, f32)
    full = (8, LANES)
    part = (4, LANES)
    result = pl.pallas_call(
        kernel,
        out_shape=jax.ShapeDtypeStruct((NY, NZ) + part, f32),
        in_specs=[pl.BlockSpec(memory_space=pl.ANY)],
        out_specs=pl.BlockSpec(memory_space=pltpu.VMEM),
        scratch_shapes=[
            vm(NY + 2 * W, NZ + 2 * W, *part),
            vm(NY + 2 * W, HZ + 2 * W, *full),
            vm(2, NY + 4, HZ + 4, *full),
            vm(NY + 2, HZ, *full),
            vm(NY, HZ + 1, *full),
            vm(NY + 2, HZ, *full),
            vm(NY, HZ, *full),
            vm(NY - 1, 3, HZ, *full),
            vm(HZ - 1, 3, NY, *full),
            vm(GROUP * GROUPS, 5, LANES),
            vm(8, 8, 5, LANES),
            vm(GZ, 5, *full),
            vm(GZ, 5, *full),
            vm(8, 8, 2, LANES),
            vm(2 * GZ + 1, *part),
            vm(GROUP * GROUPS, 2, LANES),
            vm(GZ, 3, *part),
            pltpu.SemaphoreType.DMA,
            pltpu.SemaphoreType.REGULAR,
            pltpu.SemaphoreType.REGULAR,
        ]
        + [pltpu.SemaphoreType.DMA((2,)) for _ in range(6)],
        compiler_params=pltpu.CompilerParams(
            collective_id=0, has_side_effects=True, vmem_limit_bytes=54784 * 1024
        ),
        name="diffusion_step",
    )(volume)
    return result.reshape(volume.shape)


def solution(mesh):
    placed = P("gy", "gz", None)
    return jax.shard_map(
        per_device, mesh=mesh, in_specs=(placed,), out_specs=placed, check_vma=False
    )
```

```python
import functools

import jax
import jax.numpy as jnp
from jax import lax
from jax.experimental import pallas as pl
from jax.experimental.pallas import tpu as pltpu
from jax.sharding import PartitionSpec as P

TAU = 1024.0
CONTRAST = 0.05
RATE = 0.25

NY, NZ = 8, 16
HZ = NZ // 2
W = 3
GROUP = 16
GROUPS = 4
GZ = 8
LANES = 128
MESH = pl.DeviceIdType.MESH
f32 = jnp.float32


def lane_of(v):
    return lax.broadcasted_iota(jnp.int32, v.shape, v.ndim - 1)


def piece_of(v):
    return lax.broadcasted_iota(jnp.int32, v.shape, v.ndim - 2) % 4


def x_next(v, beyond=0.0):
    r = pltpu.roll(v, LANES - 1, v.ndim - 1)
    s = pltpu.roll(r, 7, v.ndim - 2)
    s = jnp.where(piece_of(v) == 3, beyond, s)
    return jnp.where(lane_of(v) == LANES - 1, s, r)


def x_prev(v, beyond=0.0):
    r = pltpu.roll(v, 1, v.ndim - 1)
    s = pltpu.roll(r, 1, v.ndim - 2)
    s = jnp.where(piece_of(v) == 0, beyond, s)
    return jnp.where(lane_of(v) == 0, s, r)


def join(block, after):
    a, b, d, f, g = block
    a2, b2, d2, f2, g2 = after
    m = d + a2
    inv = 1.0 / (b + b2 + m)
    t, w, h = b * inv, b2 * inv, g + f2
    return (a + t * m, t * b2, d2 + w * m, f + t * h, g2 + w * h), (h * inv, t, w)


def chain(blocks):
    total, steps = blocks[0], []
    for block in blocks[1:]:
        total, step = join(total, block)
        steps.append(step)
    return total, steps


def kernel(
    vol,
    out,
    ext,
    vp,
    sm,
    cy,
    cz,
    hy,
    base,
    sav_y,
    sav_z,
    out_y,
    in_y,
    out_z,
    in_z,
    out_b,
    sep_z,
    back_y,
    back_z,
    own_sem,
    ringed,
    known,
    halo_y,
    halo_z,
    halo_o,
    sem_y,
    sem_z,
    sem_by,
    sem_bz,
):
    gy, gz = lax.axis_index("gy"), lax.axis_index("gz")
    total_y = GROUP * GROUPS
    group, place = gy // GROUP, gy % GROUP

    around = [(-1, 0), (1, 0), (-1, -1), (-1, 1), (1, -1), (1, 1), (0, -1), (0, 1)]
    ring = [8, 7, 9, 6, 10, 5, 11, 4, 12, 3, 13, 2, 14, 1, 15]
    line = [(e, d) for d in ring + [0] for e in (2, 1, 3, 0) if (e, d) != (0, 0)]

    def wrapped(x, n):
        return jnp.where(x >= n, x - n, x)

    places = [wrapped(place + d, GROUP) for d in range(GROUP)]
    groups = [wrapped(group + e, GROUPS) for e in range(GROUPS)]
    gzs = [wrapped(gz + d, GZ) for d in range(GZ)]
    gys = [gy, wrapped(gy + 1, total_y), wrapped(gy + total_y - 1, total_y)]

    def at(e, d):
        return (groups[e] * GROUP + places[d], gz)

    def send(src, dst, sems, peer):
        pltpu.make_async_remote_copy(
            src_ref=src,
            dst_ref=dst,
            send_sem=sems.at[0],
            recv_sem=sems.at[1],
            device_id=peer,
            device_id_type=MESH,
        ).start()

    def keep_own(src, dst, sems):
        pltpu.make_async_copy(src, dst, sems.at[1]).start()

    def wait(ref, sem):
        pltpu.make_async_copy(ref, ref, sem).wait()

    for t in range(4):
        pltpu.make_async_copy(
            vol.at[:, :, t * LANES : (t + 1) * LANES], ext.at[W : W + NY, W : W + NZ, t], own_sem
        ).start()

    barrier = pltpu.get_barrier_semaphore()
    peers = [(gys[i], gzs[j]) for i, j in around if i != 0]
    peers += [at(0, d % GROUP) for d in (4, -4, 3, -3, 2, -2, 1, -1)]
    peers += [(gy, gzs[d]) for d in range(1, GZ)]
    peers += [at(e, 0) for e in range(1, GROUPS)]
    for peer in peers:
        pl.semaphore_signal(barrier, inc=1, device_id=peer, device_id_type=MESH)
    wait(ext.at[W : W + NY, W : W + NZ], own_sem)
    pl.semaphore_wait(barrier, len(peers))

    def halo(i, j, src_rows, dst_rows, sems):
        src_cols = slice(NZ, NZ + W) if j > 0 else slice(W, 2 * W) if j < 0 else slice(W, W + NZ)
        dst_cols = slice(0, W) if j > 0 else slice(W + NZ, NZ + 2 * W) if j < 0 else slice(W, W + NZ)
        send(ext.at[src_rows, src_cols], ext.at[dst_rows, dst_cols], sems, (gys[i], gzs[j]))

    for i, j in around:
        if i == 0:
            halo(i, j, slice(W, W + NY), slice(W, W + NY), halo_z)
        elif i > 0:
            halo(i, j, slice(NY + 1, NY + W), slice(1, W), halo_y)
        else:
            halo(i, j, slice(W, 2 * W - 1), slice(W + NY, 2 * W + NY - 1), halo_y)
    for i, j in around:
        if i > 0:
            halo(i, j, slice(NY, NY + 1), slice(0, 1), halo_o)
        elif i < 0:
            halo(i, j, slice(2 * W - 1, 2 * W), slice(2 * W + NY - 1, 2 * W + NY), halo_o)
    for d in (4, GROUP - 4):
        pl.semaphore_signal(ringed, inc=1, device_id=at(0, d), device_id_type=MESH)

    def pack(r):
        row = ext[r]
        vp[r] = jnp.concatenate([row[: HZ + 2 * W], row[HZ:]], axis=1)

    def smooth(r):
        v = vp[r] + 2.0 * vp[r + 1] + vp[r + 2]
        v = v[:-2] + 2.0 * v[1:-1] + v[2:]
        sm[0, r] = v
        sm[1, r] = x_prev(v) + 2.0 * v + x_next(v)

    half = lax.broadcasted_iota(jnp.int32, (1, 8, LANES), 1) // 4
    low_in = jnp.where((half == 0) & (gz == 0), 0.0, 1.0).astype(f32)
    high_in = jnp.where((half == 1) & (gz == GZ - 1), 0.0, 1.0).astype(f32)

    def row_work(r, own_row, inside):
        mid = sm[1, r + 1]
        g_y = (sm[1, r + 2] - sm[1, r])[1:-1]
        g_z = mid[2:] - mid[:-2]
        core, filt = mid[1:-1], sm[0, r + 1][1:-1]
        g_x = x_next(core, filt) - x_prev(core, filt)
        yy, zz, xx = g_y * g_y, g_z * g_z, g_x * g_x
        small = f32(CONTRAST * 128.0 * 128.0)
        weight = 1.0 / (yy + zz + xx + small)
        off = weight
        if inside is not None:
            off = off * inside
        off = jnp.concatenate([off[:1] * low_in, off[1:-1], off[-1:] * high_in], axis=0)
        cy[r] = ((zz + xx + small) * weight)[1:-1]
        t_yz, t_xy = -off * g_y * g_z, -off * g_x * g_y
        v = vp[r + 2][2:-2]
        v_n = x_next(v)
        d_x = v_n - x_prev(v)
        v_z = vp[r + 2]
        d_z = (v_z[4:-2] - v_z[2:-4])
        hy[r] = t_xy[1:-1] * d_x[1:-1] + t_yz[1:-1] * d_z
        if own_row:
            t_xz = -off * g_x * g_z
            cz[r - 1] = ((yy + xx + small) * weight)[:-1]
            d_y = vp[r + 3][2:-2] - vp[r + 1][2:-2]
            k = t_xz * d_x + t_yz * d_y
            j = t_xy[1:-1] * d_y[1:-1] + t_xz[1:-1] * d_z
            t_xx = ((yy + zz + small) * weight)[1:-1]
            vc = v[1:-1]
            flux = 0.5 * (t_xx + x_next(t_xx)) * (v_n[1:-1] - vc)
            last = (lane_of(flux) == LANES - 1) & (piece_of(flux) == 3)
            flux = jnp.where(last, 0.0, flux)
            j = 0.25 * j
            change = (flux + x_next(j)) - x_prev(flux + j) + 0.25 * (k[2:] - k[:-2])
            base[r - 1] = vc + RATE * change

    def keep(cond):
        return jnp.where(cond, 0.0, 1.0).astype(f32)

    def rows(count, row, work):
        def body(n, carry):
            work(row(n))
            return carry

        lax.fori_loop(0, count, body, 0, unroll=4 if count % 4 == 0 else 2)

    def own_row(r):
        row_work(r, True, None)

    wait(ext.at[W : W + NY, 0 : 2 * W], halo_z.at[1])

    @pl.when(gz == 0)
    def _():
        ext[W : W + NY, 0:W] = jnp.zeros((NY, W, 4, LANES), f32)

    @pl.when(gz == GZ - 1)
    def _():
        ext[W : W + NY, W + NZ :] = jnp.zeros((NY, W, 4, LANES), f32)

    rows(NY, lambda n: n + W, pack)
    rows(NY - 2, lambda n: n + 3, smooth)
    rows(NY - 4, lambda n: n + 3, own_row)

    pl.semaphore_wait(ringed, 2)
    for e in range(1, GROUPS):
        pl.semaphore_signal(known, inc=1, device_id=at(e, 0), device_id_type=MESH)

    def clear(low, high):
        def zero(rows, cols):
            ext[rows, cols] = jnp.zeros((rows.stop - rows.start, cols.stop - cols.start, 4, LANES), f32)

        for rows, edge in ((low, 0), (high, total_y - 1)):

            @pl.when(gy == edge)
            def _():
                zero(rows, slice(0, NZ + 2 * W))

        for cols, edge in ((slice(0, W), 0), (slice(W + NZ, NZ + 2 * W), GZ - 1)):

            @pl.when(gz == edge)
            def _():
                zero(low, cols)
                zero(high, cols)

    wait(ext.at[0 : 2 * W - 2], halo_y.at[1])
    clear(slice(1, W), slice(W + NY, 2 * W + NY - 1))
    rows(4, lambda n: n + 1 + NY * (n // 2), pack)
    rows(4, lambda n: n + 1 + 6 * (n // 2), smooth)
    rows(4, lambda n: n + 1 + 4 * (n // 2), own_row)

    wait(ext.at[0:2], halo_o.at[1])
    clear(slice(0, 1), slice(2 * W + NY - 1, 2 * W + NY))
    for r in (0, 2 * W + NY - 1):
        pack(r)
    for r in (0, NY + 3):
        smooth(r)
    row_work(0, False, keep(gy == 0))
    row_work(NY + 1, False, keep(gy == total_y - 1))

    def reduce(first, link, right, save):
        a, b, d, f, g = jnp.zeros_like(first), first, jnp.ones_like(first), jnp.zeros_like(first), right(0)
        for s in range(1, 8):
            c = link(s)
            inv = 1.0 / (b + c + d)
            t, w = b * inv, c * inv
            save[s - 1, 0], save[s - 1, 1], save[s - 1, 2] = g * inv, t, w
            a, f = a + t * d, f + t * g
            b, d, g = t * c, 1.0 + w * d, right(s) + w * g
        return a, b, d, f, g

    def explicit(s):
        now = base[s] + (RATE * 0.25) * (hy[s + 2] - hy[s])
        base[s] = now
        return now

    first_y = TAU * (cy[0] + cy[1]) * keep(gy == 0)
    port = reduce(first_y, lambda s: TAU * (cy[s] + cy[s + 1]), explicit, sav_y)
    for c, part in enumerate(port):
        for k in range(HZ):
            out_y[4 * k : 4 * k + 4, c] = part[k, 0:4]
            out_y[4 * (k + HZ) : 4 * (k + HZ) + 4, c] = part[k, 4:8]

    mine, i8, r8 = place * 4 + group, gy // 8, gy % 8
    pl.semaphore_wait(known, GROUPS - 1)
    for e, d in line:
        send(out_y.at[places[d] * 4 + groups[e]], in_y.at[i8, r8], sem_y, at(e, d))
    keep_own(out_y.at[mine], in_y.at[i8, r8], sem_y)

    first_z = TAU * (cz[:, 0] + cz[:, 1]) * low_in
    port = reduce(first_z, lambda s: TAU * (cz[:, s] + cz[:, s + 1]), lambda s: base[:, s], sav_z)
    for c, part in enumerate(port):
        out_z[:, c] = part
    for d in range(1, GZ):
        send(out_z.at[gzs[d]], in_z.at[gz], sem_z, (gy, gzs[d]))
    keep_own(out_z.at[gz], in_z.at[gz], sem_z)

    wait(in_z, sem_z.at[1])
    blocks = [tuple(in_z[k // 2, c, 4 * (k % 2) : 4 * (k % 2) + 4] for c in range(5)) for k in range(2 * GZ)]
    whole, z_steps = chain(blocks)
    u = whole[4] / (whole[1] + whole[2])
    sep_z[0] = jnp.zeros((4, LANES), f32)
    sep_z[2 * GZ] = u
    for k in reversed(range(2 * GZ - 1)):
        h, _, w = z_steps[k]
        u = h + w * u
        sep_z[k + 1] = u
    for d in range(1, GZ):
        send(sep_z.at[pl.ds(2 * gzs[d], 3)], back_z.at[gz], sem_bz, (gy, gzs[d]))
    keep_own(sep_z.at[pl.ds(2 * gz, 3)], back_z.at[gz], sem_bz)

    wait(in_y, sem_y.at[1])
    total, steps = chain([tuple(in_y[:, i, c] for c in range(5)) for i in range(8)])
    whole, run_steps = chain([tuple(part[s : s + 1] for part in total) for s in range(8)])
    u = whole[4] / (whole[1] + whole[2])
    ends = [u]
    for h, _, w in reversed(run_steps):
        u = h + w * u
        ends.insert(0, u)
    before = jnp.concatenate([jnp.zeros((1, LANES), f32)] + ends[:-1], axis=0)
    u = jnp.concatenate(ends, axis=0)
    out_b[:, 0, 0] = before
    out_b[:, 7, 1] = u
    for i in reversed(range(7)):
        h, t, w = steps[i]
        u = h + t * before + w * u
        out_b[:, i, 1] = u
        out_b[:, i + 1, 0] = u
    halves = [(p // 8, p % 8) for p in places]
    for e, d in line:
        send(out_b.at[2 * groups[e] + halves[d][0], halves[d][1]], back_y.at[mine], sem_by, at(e, d))
    keep_own(out_b.at[i8, r8], back_y.at[mine], sem_by)

    wait(back_z, sem_bz.at[1])
    before = jnp.concatenate([back_z[:, 0], back_z[:, 1]], axis=1)
    u = jnp.concatenate([back_z[:, 1], back_z[:, 2]], axis=1)
    base[:, HZ - 1] = u
    for s in reversed(range(HZ - 1)):
        u = sav_z[s, 0] + sav_z[s, 1] * before + sav_z[s, 2] * u
        base[:, s] = u

    wait(ext.at[W : W + NY, 0 : 2 * W], halo_z.at[0])
    wait(ext.at[0 : 2 * W - 2], halo_y.at[0])
    wait(ext.at[0:2], halo_o.at[0])
    wait(out_z.at[1:], sem_z.at[0])
    wait(back_z.at[1:], sem_bz.at[0])
    wait(out_y.at[1:], sem_y.at[0])
    wait(back_y.at[1:], sem_by.at[0])

    wait(back_y, sem_by.at[1])

    def both_halves(c):
        parts = [back_y[4 * k : 4 * k + 4, c] for k in range(NZ)]
        return jnp.stack([jnp.concatenate([parts[k], parts[k + HZ]], axis=0) for k in range(HZ)])

    before, u = both_halves(0), both_halves(1)
    for s in reversed(range(NY)):
        if s < NY - 1:
            u = sav_y[s, 0] + sav_y[s, 1] * before + sav_y[s, 2] * u
        both = 0.5 * (u + base[s])
        out[s, 0:HZ] = both[:, 0:4]
        out[s, HZ:] = both[:, 4:8]


def per_device(volume):
    vm = lambda *shape: pltpu.VMEM(shape, f32)
    full = (8, LANES)
    part = (4, LANES)
    result = pl.pallas_call(
        kernel,
        out_shape=jax.ShapeDtypeStruct((NY, NZ) + part, f32),
        in_specs=[pl.BlockSpec(memory_space=pl.ANY)],
        out_specs=pl.BlockSpec(memory_space=pltpu.VMEM),
        scratch_shapes=[
            vm(NY + 2 * W, NZ + 2 * W, *part),
            vm(NY + 2 * W, HZ + 2 * W, *full),
            vm(2, NY + 4, HZ + 4, *full),
            vm(NY + 2, HZ, *full),
            vm(NY, HZ + 1, *full),
            vm(NY + 2, HZ, *full),
            vm(NY, HZ, *full),
            vm(NY - 1, 3, HZ, *full),
            vm(HZ - 1, 3, NY, *full),
            vm(GROUP * GROUPS, 5, LANES),
            vm(8, 8, 5, LANES),
            vm(GZ, 5, *full),
            vm(GZ, 5, *full),
            vm(8, 8, 2, LANES),
            vm(2 * GZ + 1, *part),
            vm(GROUP * GROUPS, 2, LANES),
            vm(GZ, 3, *part),
            pltpu.SemaphoreType.DMA,
            pltpu.SemaphoreType.REGULAR,
            pltpu.SemaphoreType.REGULAR,
        ]
        + [pltpu.SemaphoreType.DMA((2,)) for _ in range(7)],
        compiler_params=pltpu.CompilerParams(
            collective_id=0, has_side_effects=True, vmem_limit_bytes=54784 * 1024
        ),
        name="diffusion_step",
    )(volume)
    return result.reshape(volume.shape)


def solution(mesh):
    placed = P("gy", "gz", None)
    return jax.shard_map(
        per_device, mesh=mesh, in_specs=(placed,), out_specs=placed, check_vma=False
    )
```

```python
import functools

import jax
import jax.numpy as jnp
from jax import lax
from jax.experimental import pallas as pl
from jax.experimental.pallas import tpu as pltpu
from jax.sharding import PartitionSpec as P

TAU = 1024.0
CONTRAST = 0.05
RATE = 0.25

NY, NZ = 8, 16
HZ = NZ // 2
W = 3
GROUP = 16
GROUPS = 4
GZ = 8
LANES = 128
MESH = pl.DeviceIdType.MESH
f32 = jnp.float32


def lane_of(v):
    return lax.broadcasted_iota(jnp.int32, v.shape, v.ndim - 1)


def piece_of(v):
    return lax.broadcasted_iota(jnp.int32, v.shape, v.ndim - 2) % 4


def x_next(v, beyond=0.0):
    r = pltpu.roll(v, LANES - 1, v.ndim - 1)
    s = pltpu.roll(r, 7, v.ndim - 2)
    s = jnp.where(piece_of(v) == 3, beyond, s)
    return jnp.where(lane_of(v) == LANES - 1, s, r)


def x_prev(v, beyond=0.0):
    r = pltpu.roll(v, 1, v.ndim - 1)
    s = pltpu.roll(r, 1, v.ndim - 2)
    s = jnp.where(piece_of(v) == 0, beyond, s)
    return jnp.where(lane_of(v) == 0, s, r)


def join(block, after):
    a, b, d, f, g = block
    a2, b2, d2, f2, g2 = after
    m = d + a2
    inv = 1.0 / (b + b2 + m)
    t, w, h = b * inv, b2 * inv, g + f2
    return (a + t * m, t * b2, d2 + w * m, f + t * h, g2 + w * h), (h * inv, t, w)


def chain(blocks):
    total, steps = blocks[0], []
    for block in blocks[1:]:
        total, step = join(total, block)
        steps.append(step)
    return total, steps


def kernel(
    vol,
    out,
    ext,
    vp,
    sm,
    cy,
    cz,
    hy,
    base,
    sav_y,
    sav_z,
    out_y,
    in_y,
    out_z,
    in_z,
    out_b,
    sep_z,
    back_y,
    back_z,
    own_sem,
    ringed,
    known,
    halo_y,
    halo_z,
    halo_o,
    sem_y,
    sem_z,
    sem_by,
    sem_bz,
):
    gy, gz = lax.axis_index("gy"), lax.axis_index("gz")
    total_y = GROUP * GROUPS
    group, place = gy // GROUP, gy % GROUP

    around = [(-1, 0), (1, 0), (-1, -1), (-1, 1), (1, -1), (1, 1), (0, -1), (0, 1)]
    ring = [8, 7, 9, 6, 10, 5, 11, 4, 12, 3, 13, 2, 14, 1, 15]
    line = [(e, d) for d in ring + [0] for e in (2, 1, 3, 0) if (e, d) != (0, 0)]
    line.sort(key=lambda p: -min(p[0], GROUPS - p[0]) - min(p[1], GROUP - p[1]))

    def wrapped(x, n):
        return jnp.where(x >= n, x - n, x)

    places = [wrapped(place + d, GROUP) for d in range(GROUP)]
    groups = [wrapped(group + e, GROUPS) for e in range(GROUPS)]
    gzs = [wrapped(gz + d, GZ) for d in range(GZ)]
    gys = [gy, wrapped(gy + 1, total_y), wrapped(gy + total_y - 1, total_y)]

    def at(e, d):
        return (groups[e] * GROUP + places[d], gz)

    def send(src, dst, sems, peer):
        pltpu.make_async_remote_copy(
            src_ref=src,
            dst_ref=dst,
            send_sem=sems.at[0],
            recv_sem=sems.at[1],
            device_id=peer,
            device_id_type=MESH,
        ).start()

    def keep_own(src, dst, sems):
        pltpu.make_async_copy(src, dst, sems.at[1]).start()

    def wait(ref, sem):
        pltpu.make_async_copy(ref, ref, sem).wait()

    barrier = pltpu.get_barrier_semaphore()
    peers = [(gys[i], gzs[j]) for i, j in around if i != 0]
    peers += [at(0, d % GROUP) for d in (4, -4, 3, -3, 2, -2, 1, -1)]
    peers += [(gy, gzs[d]) for d in range(1, GZ)]
    peers += [at(e, 0) for e in range(1, GROUPS)]
    for peer in peers:
        pl.semaphore_signal(barrier, inc=1, device_id=peer, device_id_type=MESH)
    for t in range(4):
        pltpu.make_async_copy(
            vol.at[:, :, t * LANES : (t + 1) * LANES], ext.at[W : W + NY, W : W + NZ, t], own_sem
        ).start()

    wait(ext.at[W : W + NY, W : W + NZ], own_sem)
    pl.semaphore_wait(barrier, len(peers))

    def halo(i, j, src_rows, dst_rows, sems):
        src_cols = slice(NZ, NZ + W) if j > 0 else slice(W, 2 * W) if j < 0 else slice(W, W + NZ)
        dst_cols = slice(0, W) if j > 0 else slice(W + NZ, NZ + 2 * W) if j < 0 else slice(W, W + NZ)
        send(ext.at[src_rows, src_cols], ext.at[dst_rows, dst_cols], sems, (gys[i], gzs[j]))

    for i, j in around:
        if i == 0:
            halo(i, j, slice(W, W + NY), slice(W, W + NY), halo_z)
        elif i > 0:
            halo(i, j, slice(NY + 1, NY + W), slice(1, W), halo_y)
        else:
            halo(i, j, slice(W, 2 * W - 1), slice(W + NY, 2 * W + NY - 1), halo_y)
    for i, j in around:
        if i > 0:
            halo(i, j, slice(NY, NY + 1), slice(0, 1), halo_o)
        elif i < 0:
            halo(i, j, slice(2 * W - 1, 2 * W), slice(2 * W + NY - 1, 2 * W + NY), halo_o)
    for d in (4, GROUP - 4):
        pl.semaphore_signal(ringed, inc=1, device_id=at(0, d), device_id_type=MESH)

    def pack(r):
        row = ext[r]
        vp[r] = jnp.concatenate([row[: HZ + 2 * W], row[HZ:]], axis=1)

    def smooth(r):
        v = vp[r] + 2.0 * vp[r + 1] + vp[r + 2]
        v = v[:-2] + 2.0 * v[1:-1] + v[2:]
        sm[0, r] = v
        sm[1, r] = x_prev(v) + 2.0 * v + x_next(v)

    half = lax.broadcasted_iota(jnp.int32, (1, 8, LANES), 1) // 4
    low_in = jnp.where((half == 0) & (gz == 0), 0.0, 1.0).astype(f32)
    high_in = jnp.where((half == 1) & (gz == GZ - 1), 0.0, 1.0).astype(f32)

    def row_work(r, own_row, inside):
        mid = sm[1, r + 1]
        g_y = (sm[1, r + 2] - sm[1, r])[1:-1]
        g_z = mid[2:] - mid[:-2]
        core, filt = mid[1:-1], sm[0, r + 1][1:-1]
        g_x = x_next(core, filt) - x_prev(core, filt)
        yy, zz, xx = g_y * g_y, g_z * g_z, g_x * g_x
        small = f32(CONTRAST * 128.0 * 128.0)
        weight = 1.0 / (yy + zz + xx + small)
        off = weight
        if inside is not None:
            off = off * inside
        off = jnp.concatenate([off[:1] * low_in, off[1:-1], off[-1:] * high_in], axis=0)
        cy[r] = ((zz + xx + small) * weight)[1:-1]
        t_yz, t_xy = -off * g_y * g_z, -off * g_x * g_y
        v = vp[r + 2][2:-2]
        v_n = x_next(v)
        d_x = v_n - x_prev(v)
        v_z = vp[r + 2]
        d_z = (v_z[4:-2] - v_z[2:-4])
        hy[r] = t_xy[1:-1] * d_x[1:-1] + t_yz[1:-1] * d_z
        if own_row:
            t_xz = -off * g_x * g_z
            cz[r - 1] = ((yy + xx + small) * weight)[:-1]
            d_y = vp[r + 3][2:-2] - vp[r + 1][2:-2]
            k = t_xz * d_x + t_yz * d_y
            j = t_xy[1:-1] * d_y[1:-1] + t_xz[1:-1] * d_z
            t_xx = ((yy + zz + small) * weight)[1:-1]
            vc = v[1:-1]
            flux = 0.5 * (t_xx + x_next(t_xx)) * (v_n[1:-1] - vc)
            last = (lane_of(flux) == LANES - 1) & (piece_of(flux) == 3)
            flux = jnp.where(last, 0.0, flux)
            j = 0.25 * j
            change = (flux + x_next(j)) - x_prev(flux + j) + 0.25 * (k[2:] - k[:-2])
            base[r - 1] = vc + RATE * change

    def keep(cond):
        return jnp.where(cond, 0.0, 1.0).astype(f32)

    def rows(count, row, work):
        def body(n, carry):
            work(row(n))
            return carry

        lax.fori_loop(0, count, body, 0, unroll=4 if count % 4 == 0 else 2)

    def own_row(r):
        row_work(r, True, None)

    wait(ext.at[W : W + NY, 0 : 2 * W], halo_z.at[1])

    @pl.when(gz == 0)
    def _():
        ext[W : W + NY, 0:W] = jnp.zeros((NY, W, 4, LANES), f32)

    @pl.when(gz == GZ - 1)
    def _():
        ext[W : W + NY, W + NZ :] = jnp.zeros((NY, W, 4, LANES), f32)

    rows(NY, lambda n: n + W, pack)
    rows(NY - 2, lambda n: n + 3, smooth)
    rows(NY - 4, lambda n: n + 3, own_row)

    pl.semaphore_wait(ringed, 2)
    for e in range(1, GROUPS):
        pl.semaphore_signal(known, inc=1, device_id=at(e, 0), device_id_type=MESH)

    def clear(low, high):
        def zero(rows, cols):
            ext[rows, cols] = jnp.zeros((rows.stop - rows.start, cols.stop - cols.start, 4, LANES), f32)

        for rows, edge in ((low, 0), (high, total_y - 1)):

            @pl.when(gy == edge)
            def _():
                zero(rows, slice(0, NZ + 2 * W))

        for cols, edge in ((slice(0, W), 0), (slice(W + NZ, NZ + 2 * W), GZ - 1)):

            @pl.when(gz == edge)
            def _():
                zero(low, cols)
                zero(high, cols)

    wait(ext.at[0 : 2 * W - 2], halo_y.at[1])
    clear(slice(1, W), slice(W + NY, 2 * W + NY - 1))
    rows(4, lambda n: n + 1 + NY * (n // 2), pack)
    rows(4, lambda n: n + 1 + 6 * (n // 2), smooth)
    rows(4, lambda n: n + 1 + 4 * (n // 2), own_row)

    wait(ext.at[0:2], halo_o.at[1])
    clear(slice(0, 1), slice(2 * W + NY - 1, 2 * W + NY))
    for r in (0, 2 * W + NY - 1):
        pack(r)
    for r in (0, NY + 3):
        smooth(r)
    row_work(0, False, keep(gy == 0))
    row_work(NY + 1, False, keep(gy == total_y - 1))

    def reduce(first, link, right, save):
        a, b, d, f, g = jnp.zeros_like(first), first, jnp.ones_like(first), jnp.zeros_like(first), right(0)
        for s in range(1, 8):
            c = link(s)
            inv = 1.0 / (b + c + d)
            t, w = b * inv, c * inv
            save[s - 1, 0], save[s - 1, 1], save[s - 1, 2] = g * inv, t, w
            a, f = a + t * d, f + t * g
            b, d, g = t * c, 1.0 + w * d, right(s) + w * g
        return a, b, d, f, g

    def explicit(s):
        now = base[s] + (RATE * 0.25) * (hy[s + 2] - hy[s])
        base[s] = now
        return now

    first_y = TAU * (cy[0] + cy[1]) * keep(gy == 0)
    port = reduce(first_y, lambda s: TAU * (cy[s] + cy[s + 1]), explicit, sav_y)
    for c, part in enumerate(port):
        for k in range(HZ):
            out_y[4 * k : 4 * k + 4, c] = part[k, 0:4]
            out_y[4 * (k + HZ) : 4 * (k + HZ) + 4, c] = part[k, 4:8]

    mine, i8, r8 = place * 4 + group, gy // 8, gy % 8
    pl.semaphore_wait(known, GROUPS - 1)
    for e, d in line:
        send(out_y.at[places[d] * 4 + groups[e]], in_y.at[i8, r8], sem_y, at(e, d))
    keep_own(out_y.at[mine], in_y.at[i8, r8], sem_y)

    first_z = TAU * (cz[:, 0] + cz[:, 1]) * low_in
    port = reduce(first_z, lambda s: TAU * (cz[:, s] + cz[:, s + 1]), lambda s: base[:, s], sav_z)
    for c, part in enumerate(port):
        out_z[:, c] = part
    for d in range(1, GZ):
        send(out_z.at[gzs[d]], in_z.at[gz], sem_z, (gy, gzs[d]))
    keep_own(out_z.at[gz], in_z.at[gz], sem_z)

    wait(in_z, sem_z.at[1])
    blocks = [tuple(in_z[k // 2, c, 4 * (k % 2) : 4 * (k % 2) + 4] for c in range(5)) for k in range(2 * GZ)]
    whole, z_steps = chain(blocks)
    u = whole[4] / (whole[1] + whole[2])
    sep_z[0] = jnp.zeros((4, LANES), f32)
    sep_z[2 * GZ] = u
    for k in reversed(range(2 * GZ - 1)):
        h, _, w = z_steps[k]
        u = h + w * u
        sep_z[k + 1] = u
    for d in range(1, GZ):
        send(sep_z.at[pl.ds(2 * gzs[d], 3)], back_z.at[gz], sem_bz, (gy, gzs[d]))
    keep_own(sep_z.at[pl.ds(2 * gz, 3)], back_z.at[gz], sem_bz)

    wait(in_y, sem_y.at[1])
    total, steps = chain([tuple(in_y[:, i, c] for c in range(5)) for i in range(8)])
    whole, run_steps = chain([tuple(part[s : s + 1] for part in total) for s in range(8)])
    u = whole[4] / (whole[1] + whole[2])
    ends = [u]
    for h, _, w in reversed(run_steps):
        u = h + w * u
        ends.insert(0, u)
    before = jnp.concatenate([jnp.zeros((1, LANES), f32)] + ends[:-1], axis=0)
    u = jnp.concatenate(ends, axis=0)
    out_b[:, 0, 0] = before
    out_b[:, 7, 1] = u
    for i in reversed(range(7)):
        h, t, w = steps[i]
        u = h + t * before + w * u
        out_b[:, i, 1] = u
        out_b[:, i + 1, 0] = u
    halves = [(p // 8, p % 8) for p in places]
    for e, d in line:
        send(out_b.at[2 * groups[e] + halves[d][0], halves[d][1]], back_y.at[mine], sem_by, at(e, d))
    keep_own(out_b.at[i8, r8], back_y.at[mine], sem_by)

    wait(back_z, sem_bz.at[1])
    before = jnp.concatenate([back_z[:, 0], back_z[:, 1]], axis=1)
    u = jnp.concatenate([back_z[:, 1], back_z[:, 2]], axis=1)
    base[:, HZ - 1] = u
    for s in reversed(range(HZ - 1)):
        u = sav_z[s, 0] + sav_z[s, 1] * before + sav_z[s, 2] * u
        base[:, s] = u

    wait(ext.at[W : W + NY, 0 : 2 * W], halo_z.at[0])
    wait(ext.at[0 : 2 * W - 2], halo_y.at[0])
    wait(ext.at[0:2], halo_o.at[0])
    wait(out_z.at[1:], sem_z.at[0])
    wait(back_z.at[1:], sem_bz.at[0])
    wait(out_y.at[1:], sem_y.at[0])
    wait(back_y.at[1:], sem_by.at[0])

    wait(back_y, sem_by.at[1])

    def both_halves(c):
        parts = [back_y[4 * k : 4 * k + 4, c] for k in range(NZ)]
        return jnp.stack([jnp.concatenate([parts[k], parts[k + HZ]], axis=0) for k in range(HZ)])

    before, u = both_halves(0), both_halves(1)
    for s in reversed(range(NY)):
        if s < NY - 1:
            u = sav_y[s, 0] + sav_y[s, 1] * before + sav_y[s, 2] * u
        both = 0.5 * (u + base[s])
        out[s, 0:HZ] = both[:, 0:4]
        out[s, HZ:] = both[:, 4:8]


def per_device(volume):
    vm = lambda *shape: pltpu.VMEM(shape, f32)
    full = (8, LANES)
    part = (4, LANES)
    result = pl.pallas_call(
        kernel,
        out_shape=jax.ShapeDtypeStruct((NY, NZ) + part, f32),
        in_specs=[pl.BlockSpec(memory_space=pl.ANY)],
        out_specs=pl.BlockSpec(memory_space=pltpu.VMEM),
        scratch_shapes=[
            vm(NY + 2 * W, NZ + 2 * W, *part),
            vm(NY + 2 * W, HZ + 2 * W, *full),
            vm(2, NY + 4, HZ + 4, *full),
            vm(NY + 2, HZ, *full),
            vm(NY, HZ + 1, *full),
            vm(NY + 2, HZ, *full),
            vm(NY, HZ, *full),
            vm(NY - 1, 3, HZ, *full),
            vm(HZ - 1, 3, NY, *full),
            vm(GROUP * GROUPS, 5, LANES),
            vm(8, 8, 5, LANES),
            vm(GZ, 5, *full),
            vm(GZ, 5, *full),
            vm(8, 8, 2, LANES),
            vm(2 * GZ + 1, *part),
            vm(GROUP * GROUPS, 2, LANES),
            vm(GZ, 3, *part),
            pltpu.SemaphoreType.DMA,
            pltpu.SemaphoreType.REGULAR,
            pltpu.SemaphoreType.REGULAR,
        ]
        + [pltpu.SemaphoreType.DMA((2,)) for _ in range(7)],
        compiler_params=pltpu.CompilerParams(
            collective_id=0, has_side_effects=True, vmem_limit_bytes=54784 * 1024
        ),
        name="diffusion_step",
    )(volume)
    return result.reshape(volume.shape)


def solution(mesh):
    placed = P("gy", "gz", None)
    return jax.shard_map(
        per_device, mesh=mesh, in_specs=(placed,), out_specs=placed, check_vma=False
    )
```

```python
import functools

import jax
import jax.numpy as jnp
from jax import lax
from jax.experimental import pallas as pl
from jax.experimental.pallas import tpu as pltpu
from jax.sharding import PartitionSpec as P

TAU = 1024.0
CONTRAST = 0.05
RATE = 0.25

NY, NZ = 8, 16
HZ = NZ // 2
W = 3
GROUP = 16
GROUPS = 4
GZ = 8
LANES = 128
MESH = pl.DeviceIdType.MESH
f32 = jnp.float32


def lane_of(v):
    return lax.broadcasted_iota(jnp.int32, v.shape, v.ndim - 1)


def piece_of(v):
    return lax.broadcasted_iota(jnp.int32, v.shape, v.ndim - 2) % 4


def x_next(v, beyond=0.0):
    r = pltpu.roll(v, LANES - 1, v.ndim - 1)
    s = pltpu.roll(r, 7, v.ndim - 2)
    s = jnp.where(piece_of(v) == 3, beyond, s)
    return jnp.where(lane_of(v) == LANES - 1, s, r)


def x_prev(v, beyond=0.0):
    r = pltpu.roll(v, 1, v.ndim - 1)
    s = pltpu.roll(r, 1, v.ndim - 2)
    s = jnp.where(piece_of(v) == 0, beyond, s)
    return jnp.where(lane_of(v) == 0, s, r)


def join(block, after):
    a, b, d, f, g = block
    a2, b2, d2, f2, g2 = after
    m = d + a2
    inv = 1.0 / (b + b2 + m)
    t, w, h = b * inv, b2 * inv, g + f2
    return (a + t * m, t * b2, d2 + w * m, f + t * h, g2 + w * h), (h * inv, t, w)


def chain(blocks):
    total, steps = blocks[0], []
    for block in blocks[1:]:
        total, step = join(total, block)
        steps.append(step)
    return total, steps


def kernel(
    vol,
    out,
    ext,
    vp,
    sm,
    cy,
    cz,
    hy,
    base,
    sav_y,
    sav_z,
    out_y,
    in_y,
    out_z,
    in_z,
    out_b,
    sep_z,
    back_y,
    back_z,
    own_sem,
    ringed,
    known,
    halo_y,
    halo_z,
    halo_o,
    sem_y,
    sem_z,
    sem_by,
    sem_bz,
):
    gy, gz = lax.axis_index("gy"), lax.axis_index("gz")
    total_y = GROUP * GROUPS
    group, place = gy // GROUP, gy % GROUP

    around = [(-1, 0), (1, 0), (-1, -1), (-1, 1), (1, -1), (1, 1), (0, -1), (0, 1)]
    ring = [8, 7, 9, 6, 10, 5, 11, 4, 12, 3, 13, 2, 14, 1, 15]
    line = [(e, d) for d in ring + [0] for e in (2, 1, 3, 0) if (e, d) != (0, 0)]

    def wrapped(x, n):
        return jnp.where(x >= n, x - n, x)

    places = [wrapped(place + d, GROUP) for d in range(GROUP)]
    groups = [wrapped(group + e, GROUPS) for e in range(GROUPS)]
    gzs = [wrapped(gz + d, GZ) for d in range(GZ)]
    gys = [gy, wrapped(gy + 1, total_y), wrapped(gy + total_y - 1, total_y)]

    def at(e, d):
        return (groups[e] * GROUP + places[d], gz)

    def send(src, dst, sems, peer):
        pltpu.make_async_remote_copy(
            src_ref=src,
            dst_ref=dst,
            send_sem=sems.at[0],
            recv_sem=sems.at[1],
            device_id=peer,
            device_id_type=MESH,
        ).start()

    def keep_own(src, dst, sems):
        pltpu.make_async_copy(src, dst, sems.at[1]).start()

    def wait(ref, sem):
        pltpu.make_async_copy(ref, ref, sem).wait()

    for t in range(4):
        pltpu.make_async_copy(
            vol.at[:, :, t * LANES : (t + 1) * LANES], ext.at[W : W + NY, W : W + NZ, t], own_sem
        ).start()

    barrier = pltpu.get_barrier_semaphore()
    peers = [(gys[i], gzs[j]) for i, j in around if i != 0]
    peers += [at(0, d % GROUP) for d in (4, -4, 3, -3, 2, -2, 1, -1)]
    peers += [(gy, gzs[d]) for d in range(1, GZ)]
    peers += [at(e, 0) for e in range(1, GROUPS)]
    for peer in peers:
        pl.semaphore_signal(barrier, inc=1, device_id=peer, device_id_type=MESH)
    wait(ext.at[W : W + NY, W : W + NZ], own_sem)
    pl.semaphore_wait(barrier, len(peers))

    def halo(i, j, src_rows, dst_rows, sems):
        src_cols = slice(NZ, NZ + W) if j > 0 else slice(W, 2 * W) if j < 0 else slice(W, W + NZ)
        dst_cols = slice(0, W) if j > 0 else slice(W + NZ, NZ + 2 * W) if j < 0 else slice(W, W + NZ)
        send(ext.at[src_rows, src_cols], ext.at[dst_rows, dst_cols], sems, (gys[i], gzs[j]))

    for i, j in around:
        if i == 0:
            halo(i, j, slice(W, W + NY), slice(W, W + NY), halo_z)
        elif i > 0:
            halo(i, j, slice(NY + 1, NY + W), slice(1, W), halo_y)
        else:
            halo(i, j, slice(W, 2 * W - 1), slice(W + NY, 2 * W + NY - 1), halo_y)
    for i, j in around:
        if i > 0:
            halo(i, j, slice(NY, NY + 1), slice(0, 1), halo_o)
        elif i < 0:
            halo(i, j, slice(2 * W - 1, 2 * W), slice(2 * W + NY - 1, 2 * W + NY), halo_o)
    for d in (4, GROUP - 4):
        pl.semaphore_signal(ringed, inc=1, device_id=at(0, d), device_id_type=MESH)

    def pack(r):
        row = ext[r]
        vp[r] = jnp.concatenate([row[: HZ + 2 * W], row[HZ:]], axis=1)

    def smooth(r):
        v = vp[r] + 2.0 * vp[r + 1] + vp[r + 2]
        v = v[:-2] + 2.0 * v[1:-1] + v[2:]
        sm[0, r] = v
        sm[1, r] = x_prev(v) + 2.0 * v + x_next(v)

    half = lax.broadcasted_iota(jnp.int32, (1, 8, LANES), 1) // 4
    low_in = jnp.where((half == 0) & (gz == 0), 0.0, 1.0).astype(f32)
    high_in = jnp.where((half == 1) & (gz == GZ - 1), 0.0, 1.0).astype(f32)

    def row_work(r, own_row, inside):
        mid = sm[1, r + 1]
        g_y = (sm[1, r + 2] - sm[1, r])[1:-1]
        g_z = mid[2:] - mid[:-2]
        core, filt = mid[1:-1], sm[0, r + 1][1:-1]
        g_x = x_next(core, filt) - x_prev(core, filt)
        yy, zz, xx = g_y * g_y, g_z * g_z, g_x * g_x
        small = f32(CONTRAST * 128.0 * 128.0)
        weight = 1.0 / (yy + zz + xx + small)
        off = weight
        if inside is not None:
            off = off * inside
        off = jnp.concatenate([off[:1] * low_in, off[1:-1], off[-1:] * high_in], axis=0)
        cy[r] = ((zz + xx + small) * weight)[1:-1]
        t_yz, t_xy = -off * g_y * g_z, -off * g_x * g_y
        v = vp[r + 2][2:-2]
        v_n = x_next(v)
        d_x = v_n - x_prev(v)
        v_z = vp[r + 2]
        d_z = (v_z[4:-2] - v_z[2:-4])
        hy[r] = t_xy[1:-1] * d_x[1:-1] + t_yz[1:-1] * d_z
        if own_row:
            t_xz = -off * g_x * g_z
            cz[r - 1] = ((yy + xx + small) * weight)[:-1]
            d_y = vp[r + 3][2:-2] - vp[r + 1][2:-2]
            k = t_xz * d_x + t_yz * d_y
            j = t_xy[1:-1] * d_y[1:-1] + t_xz[1:-1] * d_z
            t_xx = ((yy + zz + small) * weight)[1:-1]
            vc = v[1:-1]
            flux = 0.5 * (t_xx + x_next(t_xx)) * (v_n[1:-1] - vc)
            last = (lane_of(flux) == LANES - 1) & (piece_of(flux) == 3)
            flux = jnp.where(last, 0.0, flux)
            j = 0.25 * j
            change = (flux + x_next(j)) - x_prev(flux + j) + 0.25 * (k[2:] - k[:-2])
            base[r - 1] = vc + RATE * change

    def keep(cond):
        return jnp.where(cond, 0.0, 1.0).astype(f32)

    def rows(count, row, work):
        def body(n, carry):
            work(row(n))
            return carry

        lax.fori_loop(0, count, body, 0, unroll=4 if count % 4 == 0 else 2)

    def own_row(r):
        row_work(r, True, None)

    wait(ext.at[W : W + NY, 0 : 2 * W], halo_z.at[1])

    @pl.when(gz == 0)
    def _():
        ext[W : W + NY, 0:W] = jnp.zeros((NY, W, 4, LANES), f32)

    @pl.when(gz == GZ - 1)
    def _():
        ext[W : W + NY, W + NZ :] = jnp.zeros((NY, W, 4, LANES), f32)

    rows(NY, lambda n: n + W, pack)
    rows(NY - 2, lambda n: n + 3, smooth)
    rows(NY - 4, lambda n: n + 3, own_row)

    pl.semaphore_wait(ringed, 2)
    for e in range(1, GROUPS):
        pl.semaphore_signal(known, inc=1, device_id=at(e, 0), device_id_type=MESH)

    def clear(low, high):
        def zero(rows, cols):
            ext[rows, cols] = jnp.zeros((rows.stop - rows.start, cols.stop - cols.start, 4, LANES), f32)

        for rows, edge in ((low, 0), (high, total_y - 1)):

            @pl.when(gy == edge)
            def _():
                zero(rows, slice(0, NZ + 2 * W))

        for cols, edge in ((slice(0, W), 0), (slice(W + NZ, NZ + 2 * W), GZ - 1)):

            @pl.when(gz == edge)
            def _():
                zero(low, cols)
                zero(high, cols)

    wait(ext.at[0 : 2 * W - 2], halo_y.at[1])
    clear(slice(1, W), slice(W + NY, 2 * W + NY - 1))
    rows(4, lambda n: n + 1 + NY * (n // 2), pack)
    rows(4, lambda n: n + 1 + 6 * (n // 2), smooth)
    rows(4, lambda n: n + 1 + 4 * (n // 2), own_row)

    wait(ext.at[0:2], halo_o.at[1])
    clear(slice(0, 1), slice(2 * W + NY - 1, 2 * W + NY))
    for r in (0, 2 * W + NY - 1):
        pack(r)
    for r in (0, NY + 3):
        smooth(r)
    row_work(0, False, keep(gy == 0))
    row_work(NY + 1, False, keep(gy == total_y - 1))

    def reduce(first, link, right, save):
        a, b, d, f, g = jnp.zeros_like(first), first, jnp.ones_like(first), jnp.zeros_like(first), right(0)
        for s in range(1, 8):
            c = link(s)
            inv = 1.0 / (b + c + d)
            t, w = b * inv, c * inv
            save[s - 1, 0], save[s - 1, 1], save[s - 1, 2] = g * inv, t, w
            a, f = a + t * d, f + t * g
            b, d, g = t * c, 1.0 + w * d, right(s) + w * g
        return a, b, d, f, g

    def explicit(s):
        now = base[s] + (RATE * 0.25) * (hy[s + 2] - hy[s])
        base[s] = now
        return now

    first_y = TAU * (cy[0] + cy[1]) * keep(gy == 0)
    port = reduce(first_y, lambda s: TAU * (cy[s] + cy[s + 1]), explicit, sav_y)
    for c, part in enumerate(port):
        for k in range(HZ):
            out_y[4 * k : 4 * k + 4, c] = part[k, 0:4]
            out_y[4 * (k + HZ) : 4 * (k + HZ) + 4, c] = part[k, 4:8]

    mine, i8, r8 = place * 4 + group, gy // 8, gy % 8
    pl.semaphore_wait(known, GROUPS - 1)
    for e, d in line:
        send(out_y.at[places[d] * 4 + groups[e]], in_y.at[i8, r8], sem_y, at(e, d))
    keep_own(out_y.at[mine], in_y.at[i8, r8], sem_y)

    first_z = TAU * (cz[:, 0] + cz[:, 1]) * low_in
    port = reduce(first_z, lambda s: TAU * (cz[:, s] + cz[:, s + 1]), lambda s: base[:, s], sav_z)
    for c, part in enumerate(port):
        out_z[:, c] = part
    for d in range(1, GZ):
        send(out_z.at[gzs[d]], in_z.at[gz], sem_z, (gy, gzs[d]))
    keep_own(out_z.at[gz], in_z.at[gz], sem_z)

    wait(in_z, sem_z.at[1])
    blocks = [tuple(in_z[k // 2, c, 4 * (k % 2) : 4 * (k % 2) + 4] for c in range(5)) for k in range(2 * GZ)]
    whole, z_steps = chain(blocks)
    u = whole[4] / (whole[1] + whole[2])
    sep_z[0] = jnp.zeros((4, LANES), f32)
    sep_z[2 * GZ] = u
    for k in reversed(range(2 * GZ - 1)):
        h, _, w = z_steps[k]
        u = h + w * u
        sep_z[k + 1] = u
    for d in range(1, GZ):
        send(sep_z.at[pl.ds(2 * gzs[d], 3)], back_z.at[gz], sem_bz, (gy, gzs[d]))
    keep_own(sep_z.at[pl.ds(2 * gz, 3)], back_z.at[gz], sem_bz)

    wait(in_y, sem_y.at[1])
    total, steps = chain([tuple(in_y[:, i, c] for c in range(5)) for i in range(8)])
    whole, run_steps = chain([tuple(part[s : s + 1] for part in total) for s in range(8)])
    u = whole[4] / (whole[1] + whole[2])
    ends = [u]
    for h, _, w in reversed(run_steps):
        u = h + w * u
        ends.insert(0, u)
    before = jnp.concatenate([jnp.zeros((1, LANES), f32)] + ends[:-1], axis=0)
    u = jnp.concatenate(ends, axis=0)
    out_b[:, 0, 0] = before
    out_b[:, 7, 1] = u
    for i in reversed(range(7)):
        h, t, w = steps[i]
        u = h + t * before + w * u
        out_b[:, i, 1] = u
        out_b[:, i + 1, 0] = u
    halves = [(p // 8, p % 8) for p in places]
    for e, d in line:
        send(out_b.at[2 * groups[e] + halves[d][0], halves[d][1]], back_y.at[mine], sem_by, at(e, d))
    keep_own(out_b.at[i8, r8], back_y.at[mine], sem_by)

    wait(back_z, sem_bz.at[1])
    before = jnp.concatenate([back_z[:, 0], back_z[:, 1]], axis=1)
    u = jnp.concatenate([back_z[:, 1], back_z[:, 2]], axis=1)
    base[:, HZ - 1] = u
    for s in reversed(range(HZ - 1)):
        u = sav_z[s, 0] + sav_z[s, 1] * before + sav_z[s, 2] * u
        base[:, s] = u

    h, t, w = sav_y[NY - 2, 0], sav_y[NY - 2, 1], sav_y[NY - 2, 2]
    for s in reversed(range(NY - 1)):
        if s < NY - 2:
            ws = sav_y[s, 2]
            h, t, w = sav_y[s, 0] + ws * h, sav_y[s, 1] + ws * t, ws * w
        base[s] = 0.5 * (base[s] + h)
        sav_y[s, 1], sav_y[s, 2] = t, w
    base[NY - 1] = 0.5 * base[NY - 1]

    wait(ext.at[W : W + NY, 0 : 2 * W], halo_z.at[0])
    wait(ext.at[0 : 2 * W - 2], halo_y.at[0])
    wait(ext.at[0:2], halo_o.at[0])
    wait(out_z.at[1:], sem_z.at[0])
    wait(back_z.at[1:], sem_bz.at[0])
    wait(out_y.at[1:], sem_y.at[0])
    wait(back_y.at[1:], sem_by.at[0])

    wait(back_y, sem_by.at[1])

    def both_halves(c):
        parts = [back_y[4 * k : 4 * k + 4, c] for k in range(NZ)]
        return jnp.stack([jnp.concatenate([parts[k], parts[k + HZ]], axis=0) for k in range(HZ)])

    before, u = 0.5 * both_halves(0), 0.5 * both_halves(1)
    for s in range(NY):
        both = base[s] + u if s == NY - 1 else base[s] + sav_y[s, 1] * before + sav_y[s, 2] * u
        out[s, 0:HZ] = both[:, 0:4]
        out[s, HZ:] = both[:, 4:8]


def per_device(volume):
    vm = lambda *shape: pltpu.VMEM(shape, f32)
    full = (8, LANES)
    part = (4, LANES)
    result = pl.pallas_call(
        kernel,
        out_shape=jax.ShapeDtypeStruct((NY, NZ) + part, f32),
        in_specs=[pl.BlockSpec(memory_space=pl.ANY)],
        out_specs=pl.BlockSpec(memory_space=pltpu.VMEM),
        scratch_shapes=[
            vm(NY + 2 * W, NZ + 2 * W, *part),
            vm(NY + 2 * W, HZ + 2 * W, *full),
            vm(2, NY + 4, HZ + 4, *full),
            vm(NY + 2, HZ, *full),
            vm(NY, HZ + 1, *full),
            vm(NY + 2, HZ, *full),
            vm(NY, HZ, *full),
            vm(NY - 1, 3, HZ, *full),
            vm(HZ - 1, 3, NY, *full),
            vm(GROUP * GROUPS, 5, LANES),
            vm(8, 8, 5, LANES),
            vm(GZ, 5, *full),
            vm(GZ, 5, *full),
            vm(8, 8, 2, LANES),
            vm(2 * GZ + 1, *part),
            vm(GROUP * GROUPS, 2, LANES),
            vm(GZ, 3, *part),
            pltpu.SemaphoreType.DMA,
            pltpu.SemaphoreType.REGULAR,
            pltpu.SemaphoreType.REGULAR,
        ]
        + [pltpu.SemaphoreType.DMA((2,)) for _ in range(7)],
        compiler_params=pltpu.CompilerParams(
            collective_id=0, has_side_effects=True, vmem_limit_bytes=54784 * 1024
        ),
        name="diffusion_step",
    )(volume)
    return result.reshape(volume.shape)


def solution(mesh):
    placed = P("gy", "gz", None)
    return jax.shard_map(
        per_device, mesh=mesh, in_specs=(placed,), out_specs=placed, check_vma=False
    )
```
